512 devices in a mesh: expert: 128 (over z, y, core), tensor: 4 (over x).
Axes of the slice: x: 4, y: 8, z: 8, core: 2. Of those that a mesh axis runs over, the one named last changes fastest.
Arguments:
- hidden_rows: bfloat16 [2048, 8, 1024], P('expert', None, 'tensor'), may hold values from -16 to 16
- route_ids: int32 [2048, 8], P('expert'), may hold values from 0 to 127, all different within a row; in each aligned block of 16 rows (0 to 15, 16 to 31, ...) at most 2 rows name the same one
- route_weights: float32 [2048, 8], P('expert'), may hold values from 0.02 to 0.25
- code_fp8: bfloat16 [128, 1024, 3584], P('expert', None, 'tensor'), may hold values from -1.875 to 1.875, as said below
- scale_fp8: float32 [128, 8, 28], P('expert', None, 'tensor'), as said below
- code_int4: bfloat16 [128, 1024, 3584], P('expert', None, 'tensor'), may hold values from -7 to 7, as said below
- scale_int4: float32 [128, 8, 3584], P('expert', None, 'tensor'), as said below
Outputs:
- mixed: bfloat16 [2048, 3584], P('expert', 'tensor')
- token_error: float32 [2048], P('expert')
- expert_ratio: float32 [128], P('expert')
The draws below stay inside these ranges and needn't reach their ends.
Inputs may be any that keep to these rules, and one draw needn't show every extreme that they name: `route_ids`: in each aligned block of 16 tokens (the tokens of one index of the expert axis), every expert is named by at most 2 routes; the 8 routes of a token name different experts; every expert is named somewhere. `code_fp8`: values of the E4M3 format: a sign times (8 + m) * 2**q / 64 with m from 0 to 7 and q from 0 to 3. `code_int4`: Integers. `scale_fp8`: Positive. `scale_int4`: Positive.
All inputs are finite; a program needn't handle non-finite values.
Results may differ from the reference program's by a relative error of at most 0.0058.
Values may be sent and summed in bfloat16 or wider, within the bound.
A program may use at most 64 MiB of HBM per device.

```python
import math
import jax
import jax.numpy as jnp
import numpy as np
from jax import lax

D = 3584
FFH = 1024
BLOCK = 128
TOPK = 8
TOK_DEV = 16
EXPERTS = 128
TOKENS = 2048
CAP = 2
N_EXPERT = 128


def block_factor(key, spread):
    uniform_draw = jax.random.uniform(jax.random.fold_in(key, 101), (EXPERTS, FFH // BLOCK, D // BLOCK), jnp.float32)
    return jnp.exp((2.0 * uniform_draw - 1.0) * spread)


def group_factor(key, spread):
    uniform_draw = jax.random.uniform(jax.random.fold_in(key, 7), (EXPERTS, FFH // BLOCK, 1), jnp.float32)
    return jnp.exp((2.0 * uniform_draw - 1.0) * spread)


def draw_code_fp8(key, part):
    key = jax.random.fold_in(key, 1)
    code_bits = jax.random.randint(key, (EXPERTS, FFH, D), 0, 64, jnp.int32)
    mantissa = code_bits % 8
    exponent = code_bits // 8 % 4
    sign_value = 1 - 2 * (code_bits // 32)
    magnitude = (8 + mantissa) * jnp.power(2, exponent)
    values = (sign_value * magnitude).astype(jnp.float32) / 64.0
    return values.astype(jnp.bfloat16)


def draw_code_int4(key, part):
    key = jax.random.fold_in(key, 2)
    values = jax.random.randint(key, (EXPERTS, FFH, D), -7, 8, jnp.int32).astype(jnp.float32)
    return values.astype(jnp.bfloat16)


def draw_scale_fp8(key, part):
    key = jax.random.fold_in(key, 3)
    factor = block_factor(key, 1.1513)
    return (factor * FFH ** (-0.5)).astype(jnp.float32)


def draw_scale_int4(key, part):
    key = jax.random.fold_in(key, 4)
    factor = group_factor(key, 1.1513)
    jitter = jnp.exp(jax.random.uniform(key, (EXPERTS, FFH // BLOCK, D), jnp.float32, -0.35, 0.35))
    return (factor * 0.25 * FFH ** (-0.5) * jitter).astype(jnp.float32)


def draw_hidden_rows(key, part):
    key = jax.random.fold_in(key, 5)
    first_key, second_key, third_key = jax.random.split(key, 3)
    base = jax.random.truncated_normal(first_key, -2.5, 2.5, (TOKENS, TOPK, FFH), jnp.float32)
    row_scale = jnp.exp(jax.random.uniform(second_key, (TOKENS, TOPK, 1, 1), jnp.float32, -1.1513, 1.1513))
    group_scale = jnp.exp(jax.random.uniform(third_key, (TOKENS, TOPK, FFH // BLOCK, 1), jnp.float32, -0.6, 0.6))
    shaped = base.reshape(TOKENS, TOPK, FFH // BLOCK, BLOCK) * row_scale * group_scale
    return shaped.reshape(TOKENS, TOPK, FFH).astype(jnp.bfloat16)


def level_of(key, dims, cuts, low, largest):
    gain = 1.0
    for axis_at, shards_of in cuts:
        steps = jax.random.uniform(jax.random.fold_in(jax.random.fold_in(key, 6), axis_at), (shards_of,), jnp.float32, low / len(cuts), largest / len(cuts))
        gain = gain * jnp.repeat(jnp.exp(steps), dims[axis_at] // shards_of).reshape((-1,) + (1,) * (len(dims) - 1 - axis_at))
    return gain


def assign_block(key, own, number, rows, number_of, top, reach, lean):
    order = jax.random.permutation(key, number_of)
    crowded, ordinary = shares(number_of, rows * top, reach, lean, True), shares(number_of, rows * top, reach, lean, False)
    places = jnp.arange(number_of)

    def named(tallies, turn):
        used = int((tallies > 0).sum())
        fixed = max(1, used // 4)
        moved = fixed + (places - fixed + turn * (used - fixed)) % max(1, number_of - fixed)
        return jnp.zeros((number_of,), jnp.int32).at[order[jnp.where(places < fixed, places, moved)]].set(jnp.asarray(tallies, jnp.int32))

    tallies = jnp.where(number % 4 == 0, named(crowded, number // 4), named(ordinary, number - number // 4 - 1))
    mixed = jax.random.permutation(jax.random.fold_in(own, 3), number_of)
    donor, receiver = mixed[0:number_of // 2 * 2:2], mixed[1:number_of // 2 * 2:2]
    room = jnp.minimum(tallies[donor] - 1, reach - tallies[receiver]) // 2
    room = jnp.where((donor == order[0]) | (receiver == order[0]) | (tallies[receiver] == 0), 0, jnp.maximum(room, 0))
    moved = jax.random.randint(jax.random.fold_in(own, 4), (number_of // 2,), 0, 1 << 20) % (room + 1)
    tallies = tallies.at[donor].add(-moved).at[receiver].add(moved)
    members = jnp.searchsorted(jnp.cumsum(tallies), jnp.arange(rows * top), side="right").astype(jnp.int32)
    grid = members.reshape(top, rows).T
    grid = grid[jax.random.permutation(jax.random.fold_in(own, 1), rows)]
    turn = jax.random.randint(jax.random.fold_in(own, 2), (rows, 1), 0, top)
    return jnp.take_along_axis(grid, (jnp.arange(top)[None, :] + turn) % top, axis=1)


def shares(number_of, total, bound, lean, full):
    weights = [(1 << 20) // math.isqrt(standing ** lean) + 1 for standing in range(1, number_of + 1)]
    largest = bound if full else min(bound, max(-(-total // number_of), total * weights[0] // sum(weights)))
    least = 1 if total - largest >= number_of - 1 else 0
    counts, surplus = [largest] + [least] * (number_of - 1), total - largest - least * (number_of - 1)
    while surplus > 0:
        candidates = [i for i in range(1, number_of) if counts[i] < largest] or [i for i in range(1, number_of) if counts[i] < bound]
        pool, budget = sum([weights[i] for i in candidates]), surplus
        for i in candidates:
            extra = min(bound - counts[i], max(1, budget * weights[i] // pool), surplus)
            counts[i] = counts[i] + extra
            surplus = surplus - extra
    return np.array(counts)


def setup_inputs(seed: int = 0) -> dict:
    seeds = jax.random.split(jax.random.key(seed), 8)
    hidden_rows = draw_hidden_rows(jax.random.fold_in(seeds[7], 71), 0)
    route_ids_keys = jax.random.split(jax.random.fold_in(seeds[1], 1), TOKENS // TOK_DEV)
    route_ids_turns = jax.random.permutation(jax.random.fold_in(seeds[1], 3), TOKENS // TOK_DEV)
    route_ids = jax.vmap(lambda own, number: assign_block(jax.random.fold_in(seeds[1], 2), own, number, TOK_DEV, EXPERTS, TOPK, CAP, 2))(route_ids_keys, route_ids_turns).reshape((TOKENS, TOPK))
    route_weights = jnp.clip(0.02 + 0.23 * jax.random.uniform(seeds[2], (TOKENS, TOPK), jnp.float32) ** level_of(seeds[2], (TOKENS, TOPK), ((0, 128),), -0.2, 0.2), 0.02, 0.25)
    code_fp8 = draw_code_fp8(jax.random.fold_in(seeds[7], 71), 0)
    scale_fp8 = draw_scale_fp8(jax.random.fold_in(seeds[7], 71), 0)
    code_int4 = draw_code_int4(jax.random.fold_in(seeds[7], 71), 0)
    scale_int4 = draw_scale_int4(jax.random.fold_in(seeds[7], 71), 0)
    return {"hidden_rows": hidden_rows, "route_ids": route_ids, "route_weights": route_weights, "code_fp8": code_fp8, "scale_fp8": scale_fp8, "code_int4": code_int4, "scale_int4": scale_int4}


def dequantize(fp8_codes, fp8_scales, int4_codes, int4_scales):
    inner, outer = fp8_codes.shape
    fp8_full = fp8_codes.astype(jnp.float32).reshape(inner // BLOCK, BLOCK, outer // BLOCK, BLOCK) * fp8_scales[:, None, :, None]
    int4_full = int4_codes.astype(jnp.float32).reshape(inner // BLOCK, BLOCK, outer) * int4_scales[:, None, :]
    return fp8_full.reshape(inner, outer).astype(jnp.bfloat16), int4_full.reshape(inner, outer).astype(jnp.bfloat16)


def reference(hidden_rows, route_ids, route_weights, code_fp8, scale_fp8, code_int4, scale_int4):
    capacity = max(2, min(TOK_DEV, (3 * TOK_DEV * TOPK + 2 * EXPERTS - 1) // (2 * EXPERTS)))
    route_count = TOKENS * TOPK
    block_ids = route_ids.reshape(N_EXPERT, TOK_DEV * TOPK)
    onehot = (block_ids[:, :, None] == jnp.arange(EXPERTS, dtype=jnp.int32)[None, None, :]).astype(jnp.int32)
    position = jnp.sum((jnp.cumsum(onehot, axis=1) - 1) * onehot, axis=2).astype(jnp.int32)
    source = jnp.arange(N_EXPERT, dtype=jnp.int32)[:, None]
    slot_index = block_ids * (N_EXPERT * capacity) + source * capacity + position
    table = jnp.full((EXPERTS * N_EXPERT * capacity,), route_count, jnp.int32)
    table = table.at[slot_index.reshape(-1)].set(jnp.arange(route_count, dtype=jnp.int32))
    table = table.reshape(EXPERTS, N_EXPERT * capacity)
    hidden_flat = jnp.concatenate([hidden_rows.reshape(route_count, FFH), jnp.zeros((1, FFH), jnp.bfloat16)], axis=0)
    weight_flat = jnp.concatenate([route_weights.reshape(-1), jnp.zeros((1,), jnp.float32)])
    token_flat = jnp.concatenate([jnp.arange(route_count, dtype=jnp.int32) // TOPK, jnp.full((1,), TOKENS, jnp.int32)])

    def per_expert(carry, items):
        mixed_sum, error_sum = carry
        index, fp8_codes, fp8_scales, int4_codes, int4_scales = items
        weight_fp8, weight_int4 = dequantize(fp8_codes, fp8_scales, int4_codes, int4_scales)
        routed = hidden_flat[index]
        fp8_low = lax.optimization_barrier(jnp.dot(routed, weight_fp8, preferred_element_type=jnp.float32).astype(jnp.bfloat16))
        int4_low = lax.optimization_barrier(jnp.dot(routed, weight_int4, preferred_element_type=jnp.float32).astype(jnp.bfloat16))
        fp8_value = fp8_low.astype(jnp.float32)
        deviation = int4_low.astype(jnp.float32) - fp8_value
        route_error = jnp.sum(deviation * deviation, axis=1)
        gate_value = weight_flat[index]
        owner = token_flat[index]
        mixed_sum = mixed_sum.at[owner].add(gate_value[:, None] * fp8_value)
        error_sum = error_sum.at[owner].add(gate_value * route_error)
        ratio = jnp.sum(route_error) / (jnp.sum(fp8_value * fp8_value) + 1e-6)
        return (mixed_sum, error_sum), ratio

    start = (jnp.zeros((TOKENS + 1, D), jnp.float32), jnp.zeros((TOKENS + 1,), jnp.float32))
    (mixed_sum, error_sum), ratios = lax.scan(per_expert, start, (table, code_fp8, scale_fp8, code_int4, scale_int4))
    return mixed_sum[:TOKENS].astype(jnp.bfloat16), error_sum[:TOKENS], ratios
```

```python
import functools

import jax
import jax.numpy as jnp
from jax import lax
from jax.experimental import pallas as pl
from jax.experimental.pallas import tpu as pltpu
from jax.sharding import PartitionSpec as P

BLOCK = 128
SLOTS = 2
COLUMN = 8
MESH = pl.DeviceIdType.MESH
f32, bf16 = jnp.float32, jnp.bfloat16


def iota(shape, dim):
    return lax.broadcasted_iota(jnp.int32, shape, dim)


def dot(a, b):
    return jnp.dot(a, b, preferred_element_type=f32)


def split3(value):
    high = value.astype(bf16).astype(f32)
    rest = value - high
    middle = rest.astype(bf16).astype(f32)
    return high, middle, rest - middle


def chunks_of(width):
    full = 2 * BLOCK
    starts = list(range(0, width, full))
    return [(s, min(full, width - s)) for s in starts]


def kernel(
    sizes,
    ids_ref, gate_ref, hidden_ref, scale8_ref, scale4_ref, code8_ref, code4_ref,
    mixed_ref, token_ref, ratio_ref,
    w8, w4, send1, gates1, recv1, grecv, send2, x_all, out8, back1, part, back2, sums, sums_all,
    code_sem, s1, r1, sg, rg, s2, r2, sx, rx, se, re, sb, rb, sc, rc,
):
    zs, rs, xs, tok, top = sizes
    routes = tok * top
    rows = zs * rs * SLOTS
    z_rows, r_rows = rs * SLOTS, zs * SLOTS
    width = hidden_ref.shape[1]
    inner, feats = w8.shape
    chunks = chunks_of(feats)

    me, tn = lax.axis_index("expert"), lax.axis_index("tensor")
    z, r = me // rs, lax.rem(me, rs)

    def in_column(d):
        return lax.rem(z + d, zs)

    def in_row(d):
        return lax.rem(r + d, rs)

    def in_gather(d):
        return lax.rem(tn + d, xs)

    part_rows = inner // 2
    code_copies = []
    for n, (src, dst) in enumerate(((code8_ref, w8), (code4_ref, w4))):
        for h in range(2):
            piece = pl.ds(h * part_rows, part_rows)
            copy = pltpu.make_async_copy(src.at[0, piece, :], dst.at[piece, :], code_sem.at[n, h])
            copy.start()
            code_copies.append(copy)

    barrier = pltpu.get_barrier_semaphore()

    @pl.loop(1, zs)
    def _(d):
        pl.semaphore_signal(
            barrier, inc=1, device_id={"expert": in_column(d) * rs + r}, device_id_type=MESH
        )

    @pl.loop(1, rs)
    def _(d):
        pl.semaphore_signal(
            barrier, inc=1, device_id={"expert": z * rs + in_row(d)}, device_id_type=MESH
        )

    @pl.loop(1, xs)
    def _(d):
        pl.semaphore_signal(barrier, inc=1, device_id={"tensor": in_gather(d)}, device_id_type=MESH)

    ids = jnp.broadcast_to(ids_ref[...], (routes, routes))
    earlier = (ids == ids.T) & (iota((routes, routes), 0) < iota((routes, routes), 1))
    position = jnp.sum(earlier.astype(jnp.int32), axis=0, keepdims=True)
    target = ids_ref[...] * SLOTS + position
    chosen = iota((rows, routes), 0) == target
    select = chosen.astype(f32).astype(bf16)
    gate = gate_ref[...]
    gate_high = gate.astype(bf16).astype(f32)
    gate_low = gate - gate_high
    lanes = gates1.shape[1]
    token_of = iota((routes, lanes), 0) // top
    place = iota((routes, lanes), 1)
    spread_high = (place == token_of).astype(f32).astype(bf16)
    spread_low = (place == token_of + tok).astype(f32).astype(bf16)
    send1[...] = dot(select, hidden_ref[...]).astype(bf16)
    gates1[...] = (
        dot(jnp.where(chosen, gate_high, 0.0).astype(bf16), spread_high)
        + dot(jnp.where(chosen, gate_low, 0.0).astype(bf16), spread_low)
    ).astype(bf16)

    pl.semaphore_wait(barrier, zs + rs + xs - 3)

    def column_copy(src, dst, there, send, recv):
        return pltpu.make_async_remote_copy(
            src_ref=src,
            dst_ref=dst,
            send_sem=send,
            recv_sem=recv,
            device_id={"expert": there * rs + r},
            device_id_type=MESH,
        )

    def row_copy(src, dst, there, send, recv):
        return pltpu.make_async_remote_copy(
            src_ref=src,
            dst_ref=dst,
            send_sem=send,
            recv_sem=recv,
            device_id={"expert": z * rs + there},
            device_id_type=MESH,
        )

    def gather_copy(src, dst, there, send, recv):
        return pltpu.make_async_remote_copy(
            src_ref=src,
            dst_ref=dst,
            send_sem=send,
            recv_sem=recv,
            device_id={"tensor": there},
            device_id_type=MESH,
        )

    def z_block(n):
        return pl.ds(pl.multiple_of(n * z_rows, z_rows), z_rows)

    def r_block(n):
        return pl.ds(pl.multiple_of(n * r_rows, r_rows), r_rows)

    def t_block(n):
        return pl.ds(pl.multiple_of(n * tok, tok), tok)

    @pl.loop(1, zs)
    def _(d):
        there = in_column(d)
        column_copy(send1.at[z_block(there)], recv1.at[z_block(z)], there, s1, r1).start()

    @pl.loop(1, zs)
    def _(d):
        there = in_column(d)
        column_copy(gates1.at[z_block(there)], grecv.at[z_block(z)], there, sg, rg).start()

    recv1[z_block(z), :] = send1[z_block(z), :]
    grecv[z_block(z), :] = gates1[z_block(z), :]

    def scale_weights(first, last):
        @pl.loop(first, last)
        def _(g):
            group = pl.ds(pl.multiple_of(g * BLOCK, BLOCK), BLOCK)
            for b in range(feats // BLOCK):
                cols = pl.ds(b * BLOCK, BLOCK)
                w8[group, cols] = (w8[group, cols].astype(f32) * scale8_ref[0, g, b]).astype(bf16)
            w4[group, :] = (w4[group, :].astype(f32) * scale4_ref[0, pl.ds(g, 1), :]).astype(bf16)

    groups = inner // BLOCK
    for copy in code_copies:
        copy.wait()
    scale_weights(0, groups // 4)

    at, of = iota((rows, rows), 0), iota((rows, rows), 1)
    reorder = of == (at % r_rows) // SLOTS * z_rows + at // r_rows * SLOTS + at % SLOTS
    reorder = reorder.astype(f32).astype(bf16)

    all_but_one = pl.ds(0, rows - z_rows)
    wait = column_copy(send1.at[all_but_one], recv1.at[all_but_one], z, s1, r1)
    wait.wait_recv()
    send2[...] = dot(reorder, recv1[...]).astype(bf16)

    mine = pl.ds(pl.multiple_of(tn * width, width), width)

    @pl.loop(1, rs)
    def _(d):
        there = in_row(d)
        row_copy(send2.at[r_block(there)], x_all.at[r_block(r), mine], there, s2, r2).start()

    x_all[r_block(r), mine] = send2[r_block(r), :]

    wait_g = column_copy(gates1.at[all_but_one], grecv.at[all_but_one], z, sg, rg)
    wait_g.wait_recv()
    tokens = zs * tok
    gates = dot(reorder, grecv[...]).astype(bf16)
    lane, wide = iota((lanes, 2 * tokens), 0), iota((lanes, 2 * tokens), 1)
    widen = (lane == wide % tok + jnp.where(wide < tokens, 0, tok)).astype(f32).astype(bf16)
    wide_gates = dot(gates, widen)
    row_z = iota((rows, 2 * tokens), 0) % r_rows // SLOTS
    lane_z = iota((rows, 2 * tokens), 1) % tokens // tok
    combine = jnp.where(row_z == lane_z, wide_gates, 0.0).T.astype(bf16)

    scale_weights(groups // 4, groups // 2)

    all_but_r = pl.ds(0, rows - r_rows)
    wait_2 = row_copy(send2.at[all_but_r], x_all.at[all_but_r, mine], r, s2, r2)
    wait_2.wait_recv()

    @pl.loop(1, xs)
    def _(d):
        gather_copy(x_all.at[:, mine], x_all.at[:, mine], in_gather(d), sx, rx).start()

    scale_weights(groups // 2, groups)
    others = pl.ds(0, (xs - 1) * width)
    wait_x = gather_copy(x_all.at[:, others], x_all.at[:, others], tn, sx, rx)
    wait_x.wait_recv()

    def send_back(c):
        @pl.loop(1, rs)
        def _(d):
            there = in_row(d)
            row_copy(
                out8.at[c, r_block(there)], back1.at[c, r_block(r)], there, sb.at[c], rb.at[c]
            ).start()

        back1[c, r_block(r), :] = out8[c, r_block(r), :]

    last = len(chunks) - 1
    for c, (start, size) in enumerate(chunks):
        out8[c, :, :size] = dot(x_all[...], w8[:, start : start + size]).astype(bf16)
        if c < last:
            send_back(c)
    gap_sum = jnp.zeros((rows, BLOCK), f32)
    ref_sum = jnp.zeros((rows, BLOCK), f32)
    for c, (start, size) in enumerate(chunks):
        result4 = dot(x_all[...], w4[:, start : start + size]).astype(bf16).astype(f32)
        result8 = out8[c, :, :size].astype(f32)
        gap = result4 - result8
        for b in range(size // BLOCK):
            cols = slice(b * BLOCK, (b + 1) * BLOCK)
            gap_sum += gap[:, cols] * gap[:, cols]
            ref_sum += result8[:, cols] * result8[:, cols]

    gap_row = jnp.sum(gap_sum.T, axis=0, keepdims=True)
    ref_row = jnp.sum(ref_sum.T, axis=0, keepdims=True)
    which = iota((8, rows), 0)
    sums[...] = jnp.where(which == 0, gap_row, jnp.where(which == 1, ref_row, 0.0))
    sums_all[tn] = sums[...]

    @pl.loop(1, xs)
    def _(d):
        gather_copy(sums, sums_all.at[tn], in_gather(d), se, re).start()

    def combine_and_send(c):
        wait_b = row_copy(
            out8.at[c, all_but_r], back1.at[c, all_but_r], r, sb.at[c], rb.at[c]
        )
        wait_b.wait_recv()
        both = dot(combine, back1[c])
        total = both[:tokens] + both[tokens:]
        if c == last:
            size = chunks[c][1]
            error = jnp.sum(total[:, size:], axis=1, keepdims=True)
            high, middle, low = split3(error)
            lane = iota((tokens, BLOCK), 1)
            parts = jnp.where(
                lane == 0, high, jnp.where(lane == 1, middle, jnp.where(lane == 2, low, 0.0))
            )
            part[c, :, :size] = total[:, :size].astype(bf16)
            part[c, :, size:] = parts.astype(bf16)
        else:
            part[c] = total.astype(bf16)

        @pl.loop(1, zs)
        def _(d):
            there = in_column(d)
            column_copy(
                part.at[c, t_block(there)], back2.at[c, t_block(z)], there, sc.at[c], rc.at[c]
            ).start()

        back2[c, t_block(z), :] = part[c, t_block(z), :]

    if last > 0:
        combine_and_send(0)

    sums_but = pl.ds(0, xs - 1)
    wait_e = pltpu.make_async_remote_copy(
        src_ref=sums_all.at[sums_but],
        dst_ref=sums_all.at[sums_but],
        send_sem=se,
        recv_sem=re,
        device_id={"tensor": tn},
        device_id_type=MESH,
    )
    wait_e.wait_recv()
    total = sums_all[0]
    for n in range(1, xs):
        total = total + sums_all[n]
    gap_total, ref_total = total[0:1], total[1:2]
    ratio_ref[...] = jnp.sum(gap_total, axis=1, keepdims=True) / (
        jnp.sum(ref_total, axis=1, keepdims=True) + 1e-06
    )
    high, middle, low = split3(gap_total)
    which = iota((BLOCK, rows), 0)
    stacked = jnp.where(
        which == 0, high, jnp.where(which == 1, middle, jnp.where(which == 2, low, 0.0))
    )
    size = chunks[last][1]
    out8[last, :, size:] = stacked.T.astype(bf16)
    send_back(last)

    for c in range(1, last + 1):
        combine_and_send(c)

    all_but_t = pl.ds(0, tokens - tok)
    for c, (start, size) in enumerate(chunks):
        wait_c = column_copy(part.at[c, all_but_t], back2.at[c, all_but_t], z, sc.at[c], rc.at[c])
        wait_c.wait_recv()
        total = back2[c, :tok].astype(f32)
        for n in range(1, zs):
            total = total + back2[c, n * tok : (n + 1) * tok].astype(f32)
        mixed_ref[:, start : start + size] = total[:, :size].astype(bf16)
        if c == last:
            error = jnp.sum(total[:, size:], axis=1, keepdims=True)
            diagonal = iota((tok, tok), 0) == iota((tok, tok), 1)
            token_ref[...] = jnp.sum(jnp.where(diagonal, error, 0.0), axis=0, keepdims=True)

    wait.wait_send()
    wait_g.wait_send()
    wait_2.wait_send()
    wait_x.wait_send()
    wait_e.wait_send()
    for c in range(len(chunks)):
        row_copy(
            out8.at[c, all_but_r], back1.at[c, all_but_r], r, sb.at[c], rb.at[c]
        ).wait_send()
        column_copy(
            part.at[c, all_but_t], back2.at[c, all_but_t], z, sc.at[c], rc.at[c]
        ).wait_send()


def per_device(sizes, hidden, ids, gates, code8, scale8, code4, scale4):
    zs, rs, xs, tok, top = sizes
    routes, width = tok * top, hidden.shape[2]
    rows = zs * rs * SLOTS
    inner, feats = code8.shape[1:]
    chunks = chunks_of(feats)
    count, tokens = len(chunks), zs * tok
    wide = max(chunks[-1][1] + BLOCK, chunks[0][1])
    vmem, smem = pl.BlockSpec(memory_space=pltpu.VMEM), pl.BlockSpec(memory_space=pltpu.SMEM)
    dma = pltpu.SemaphoreType.DMA
    mixed, token, ratio = pl.pallas_call(
        functools.partial(kernel, sizes),
        out_shape=(
            jax.ShapeDtypeStruct((tok, feats), bf16),
            jax.ShapeDtypeStruct((1, tok), f32),
            jax.ShapeDtypeStruct((1, 1), f32),
        ),
        in_specs=[vmem, vmem, vmem, smem, vmem]
        + [pl.BlockSpec(memory_space=pl.ANY)] * 2,
        out_specs=(vmem, vmem, vmem),
        scratch_shapes=[
            pltpu.VMEM((inner, feats), bf16),
            pltpu.VMEM((inner, feats), bf16),
            pltpu.VMEM((rows, width), bf16),
            pltpu.VMEM((rows, BLOCK), bf16),
            pltpu.VMEM((rows, width), bf16),
            pltpu.VMEM((rows, BLOCK), bf16),
            pltpu.VMEM((rows, width), bf16),
            pltpu.VMEM((rows, xs * width), bf16),
            pltpu.VMEM((count, rows, wide), bf16),
            pltpu.VMEM((count, rows, wide), bf16),
            pltpu.VMEM((count, tokens, wide), bf16),
            pltpu.VMEM((count, tokens, wide), bf16),
            pltpu.VMEM((8, rows), f32),
            pltpu.VMEM((xs, 8, rows), f32),
            dma((2, 2)),
        ]
        + [dma] * 10
        + [dma((count,))] * 4,
        compiler_params=pltpu.CompilerParams(
            collective_id=0, has_side_effects=True, vmem_limit_bytes=32 * 1024 * 1024
        ),
    )(
        ids.reshape(1, routes),
        gates.reshape(1, routes),
        hidden.reshape(routes, width),
        scale8,
        scale4,
        code8,
        code4,
    )
    return mixed, token.reshape(tok), ratio.reshape(1)


def solution(mesh):
    experts, xs = mesh.shape["expert"], mesh.shape["tensor"]
    zs = COLUMN
    rs = experts // zs

    def run(hidden, *rest):
        tok, top = hidden.shape[0] // experts, hidden.shape[1]
        mapped = jax.shard_map(
            functools.partial(per_device, (zs, rs, xs, tok, top)),
            mesh=mesh,
            in_specs=(
                P("expert", None, "tensor"),
                P("expert", None),
                P("expert", None),
                P("expert", None, "tensor"),
                P("expert", None, "tensor"),
                P("expert", None, "tensor"),
                P("expert", None, "tensor"),
            ),
            out_specs=(P("expert", "tensor"), P("expert"), P("expert")),
            check_vma=False,
        )
        return mapped(hidden, *rest)

    return run
```

```python
import functools

import jax
import jax.numpy as jnp
from jax import lax
from jax.experimental import pallas as pl
from jax.experimental.pallas import tpu as pltpu
from jax.sharding import PartitionSpec as P

BLOCK = 128
SLOTS = 2
COLUMN = 8
MESH = pl.DeviceIdType.MESH
f32, bf16 = jnp.float32, jnp.bfloat16


def iota(shape, dim):
    return lax.broadcasted_iota(jnp.int32, shape, dim)


def dot(a, b):
    return jnp.dot(a, b, preferred_element_type=f32)


def split3(value):
    high = value.astype(bf16).astype(f32)
    rest = value - high
    middle = rest.astype(bf16).astype(f32)
    return high, middle, rest - middle


def chunks_of(width):
    full = 2 * BLOCK
    starts = list(range(0, width, full))
    return [(s, min(full, width - s)) for s in starts]


def kernel(
    sizes,
    ids_hbm, gate_hbm, hidden_hbm, scale8_hbm, scale4_hbm, code8_hbm, code4_hbm,
    mixed_ref, token_ref, ratio_ref,
    ids_ref, gate_ref, hidden_ref, scale8_ref, scale4_ref, w8, w4, send1, gates1, recv1, grecv, send2, x_all, out8, back1, part, back2, sums, sums_all,
    small_sem, code_sem, s1, r1, sg, rg, s2, r2, sx, rx, se, re, sb, rb, sc, rc,
):
    zs, rs, xs, tok, top = sizes
    routes = tok * top
    rows = zs * rs * SLOTS
    z_rows, r_rows = rs * SLOTS, zs * SLOTS
    width = hidden_ref.shape[1]
    inner, feats = w8.shape
    chunks = chunks_of(feats)

    me, tn = lax.axis_index("expert"), lax.axis_index("tensor")
    z, r = me // rs, lax.rem(me, rs)

    def far_first(d, count):
        step = d // 2
        return count // 2 + jnp.where(d % 2 == 1, -step, step)

    def in_column(d):
        return lax.rem(z + far_first(d, zs), zs)

    def in_row(d):
        return lax.rem(r + far_first(d, rs), rs)

    def in_gather(d):
        return lax.rem(tn + d, xs)

    small = (
        (ids_hbm, ids_ref),
        (gate_hbm, gate_ref),
        (hidden_hbm, hidden_ref),
        (scale8_hbm, scale8_ref),
        (scale4_hbm, scale4_ref),
    )
    small_copies = []
    for n, (src, dst) in enumerate(small):
        copy = pltpu.make_async_copy(src, dst, small_sem.at[n])
        copy.start()
        small_copies.append(copy)

    barrier = pltpu.get_barrier_semaphore()

    @pl.loop(1, zs)
    def _(d):
        pl.semaphore_signal(
            barrier, inc=1, device_id={"expert": in_column(d) * rs + r}, device_id_type=MESH
        )

    @pl.loop(1, rs)
    def _(d):
        pl.semaphore_signal(
            barrier, inc=1, device_id={"expert": z * rs + in_row(d)}, device_id_type=MESH
        )

    @pl.loop(1, xs)
    def _(d):
        pl.semaphore_signal(barrier, inc=1, device_id={"tensor": in_gather(d)}, device_id_type=MESH)

    part_rows = inner // 2
    code_copies = []
    for n, (src, dst) in enumerate(((code8_hbm, w8), (code4_hbm, w4))):
        for h in range(2):
            piece = pl.ds(h * part_rows, part_rows)
            copy = pltpu.make_async_copy(src.at[0, piece, :], dst.at[piece, :], code_sem.at[n, h])
            copy.start()
            code_copies.append(copy)

    for copy in small_copies[:3]:
        copy.wait()
    gate = gate_ref[...]
    high = gate.astype(bf16).astype(f32)
    table = jnp.concatenate([ids_ref[...].astype(f32), high, gate - high], axis=0).astype(bf16)
    repeat = (iota((tok, routes), 0) == iota((tok, routes), 1) // top).astype(f32).astype(bf16)
    table = dot(table, repeat)
    own_choice = iota((top, routes), 0) == iota((top, routes), 1) % top

    def flat(n):
        rows_of = table[n * top : (n + 1) * top]
        return jnp.sum(jnp.where(own_choice, rows_of, 0.0), axis=0, keepdims=True)

    flat_ids, gate_high, gate_low = flat(0), flat(1), flat(2)
    ids = jnp.broadcast_to(flat_ids, (routes, routes))
    earlier = (ids == ids.T) & (iota((routes, routes), 0) < iota((routes, routes), 1))
    position = jnp.sum(jnp.where(earlier, 1.0, 0.0), axis=0, keepdims=True)
    target = (flat_ids * SLOTS + position).astype(jnp.int32)
    chosen = iota((rows, routes), 0) == target
    select = chosen.astype(f32).astype(bf16)
    lanes = gates1.shape[1]
    token_of = iota((routes, lanes), 0) // top
    place = iota((routes, lanes), 1)
    spread_high = (place == token_of).astype(f32).astype(bf16)
    spread_low = (place == token_of + tok).astype(f32).astype(bf16)
    send1[...] = dot(select, hidden_ref[...]).astype(bf16)
    gates1[...] = (
        dot(jnp.where(chosen, gate_high, 0.0).astype(bf16), spread_high)
        + dot(jnp.where(chosen, gate_low, 0.0).astype(bf16), spread_low)
    ).astype(bf16)

    pl.semaphore_wait(barrier, zs + rs + xs - 3)

    def column_copy(src, dst, there, send, recv):
        return pltpu.make_async_remote_copy(
            src_ref=src,
            dst_ref=dst,
            send_sem=send,
            recv_sem=recv,
            device_id={"expert": there * rs + r},
            device_id_type=MESH,
        )

    def row_copy(src, dst, there, send, recv):
        return pltpu.make_async_remote_copy(
            src_ref=src,
            dst_ref=dst,
            send_sem=send,
            recv_sem=recv,
            device_id={"expert": z * rs + there},
            device_id_type=MESH,
        )

    def gather_copy(src, dst, there, send, recv):
        return pltpu.make_async_remote_copy(
            src_ref=src,
            dst_ref=dst,
            send_sem=send,
            recv_sem=recv,
            device_id={"tensor": there},
            device_id_type=MESH,
        )

    def z_block(n):
        return pl.ds(pl.multiple_of(n * z_rows, z_rows), z_rows)

    def r_block(n):
        return pl.ds(pl.multiple_of(n * r_rows, r_rows), r_rows)

    def t_block(n):
        return pl.ds(pl.multiple_of(n * tok, tok), tok)

    @pl.loop(1, zs)
    def _(d):
        there = in_column(d)
        column_copy(send1.at[z_block(there)], recv1.at[z_block(z)], there, s1, r1).start()

    recv1[z_block(z), :] = send1[z_block(z), :]
    grecv[z_block(z), :] = gates1[z_block(z), :]

    def scale_weights(first, last):
        @pl.loop(first, last)
        def _(g):
            group = pl.ds(pl.multiple_of(g * BLOCK, BLOCK), BLOCK)
            for b in range(feats // BLOCK):
                cols = pl.ds(b * BLOCK, BLOCK)
                w8[group, cols] = (w8[group, cols].astype(f32) * scale8_ref[b, 0, g]).astype(bf16)
            w4[group, :] = (w4[group, :].astype(f32) * scale4_ref[0, pl.ds(g, 1), :]).astype(bf16)

    groups = inner // BLOCK
    for copy in small_copies[3:] + code_copies:
        copy.wait()
    scale_weights(0, groups // 4)

    at, of = iota((rows, rows), 0), iota((rows, rows), 1)
    reorder = of == (at % r_rows) // SLOTS * z_rows + at // r_rows * SLOTS + at % SLOTS
    reorder = reorder.astype(f32).astype(bf16)

    all_but_one = pl.ds(0, rows - z_rows)
    wait = column_copy(send1.at[all_but_one], recv1.at[all_but_one], z, s1, r1)
    wait.wait_recv()
    send2[...] = dot(reorder, recv1[...]).astype(bf16)

    mine = pl.ds(pl.multiple_of(tn * width, width), width)

    @pl.loop(1, rs)
    def _(d):
        there = in_row(d)
        row_copy(send2.at[r_block(there)], x_all.at[r_block(r), mine], there, s2, r2).start()

    @pl.loop(1, zs)
    def _(d):
        there = in_column(d)
        column_copy(gates1.at[z_block(there)], grecv.at[z_block(z)], there, sg, rg).start()

    x_all[r_block(r), mine] = send2[r_block(r), :]

    scale_weights(groups // 4, groups // 2)

    all_but_r = pl.ds(0, rows - r_rows)
    wait_2 = row_copy(send2.at[all_but_r], x_all.at[all_but_r, mine], r, s2, r2)
    wait_2.wait_recv()

    @pl.loop(1, xs)
    def _(d):
        gather_copy(x_all.at[:, mine], x_all.at[:, mine], in_gather(d), sx, rx).start()

    wait_g = column_copy(gates1.at[all_but_one], grecv.at[all_but_one], z, sg, rg)
    wait_g.wait_recv()
    tokens = zs * tok
    gates = dot(reorder, grecv[...]).astype(bf16)
    lane, wide = iota((lanes, 2 * tokens), 0), iota((lanes, 2 * tokens), 1)
    widen = (lane == wide % tok + jnp.where(wide < tokens, 0, tok)).astype(f32).astype(bf16)
    wide_gates = dot(gates, widen)
    row_z = iota((rows, 2 * tokens), 0) % r_rows // SLOTS
    lane_z = iota((rows, 2 * tokens), 1) % tokens // tok
    combine = jnp.where(row_z == lane_z, wide_gates, 0.0).T.astype(bf16)

    scale_weights(groups // 2, groups)
    others = pl.ds(0, (xs - 1) * width)
    wait_x = gather_copy(x_all.at[:, others], x_all.at[:, others], tn, sx, rx)
    wait_x.wait_recv()

    def send_back(c):
        @pl.loop(1, rs)
        def _(d):
            there = in_row(d)
            row_copy(
                out8.at[c, r_block(there)], back1.at[c, r_block(r)], there, sb.at[c], rb.at[c]
            ).start()

        back1[c, r_block(r), :] = out8[c, r_block(r), :]

    last = len(chunks) - 1
    for c, (start, size) in enumerate(chunks):
        out8[c, :, :size] = dot(x_all[...], w8[:, start : start + size]).astype(bf16)
        if c < last:
            send_back(c)
    gap_sum = jnp.zeros((rows, BLOCK), f32)
    ref_sum = jnp.zeros((rows, BLOCK), f32)
    for c, (start, size) in enumerate(chunks):
        result4 = dot(x_all[...], w4[:, start : start + size]).astype(bf16).astype(f32)
        result8 = out8[c, :, :size].astype(f32)
        gap = result4 - result8
        for b in range(size // BLOCK):
            cols = slice(b * BLOCK, (b + 1) * BLOCK)
            gap_sum += gap[:, cols] * gap[:, cols]
            ref_sum += result8[:, cols] * result8[:, cols]

    gap_row = jnp.sum(gap_sum.T, axis=0, keepdims=True)
    ref_row = jnp.sum(ref_sum.T, axis=0, keepdims=True)
    which = iota((8, rows), 0)
    sums[...] = jnp.where(which == 0, gap_row, jnp.where(which == 1, ref_row, 0.0))
    sums_all[tn] = sums[...]

    @pl.loop(1, xs)
    def _(d):
        gather_copy(sums, sums_all.at[tn], in_gather(d), se, re).start()

    def combine_and_send(c):
        wait_b = row_copy(
            out8.at[c, all_but_r], back1.at[c, all_but_r], r, sb.at[c], rb.at[c]
        )
        wait_b.wait_recv()
        both = dot(combine, back1[c])
        total = both[:tokens] + both[tokens:]
        if c == last:
            size = chunks[c][1]
            error = jnp.sum(total[:, size:], axis=1, keepdims=True)
            high, middle, low = split3(error)
            lane = iota((tokens, BLOCK), 1)
            parts = jnp.where(
                lane == 0, high, jnp.where(lane == 1, middle, jnp.where(lane == 2, low, 0.0))
            )
            part[c, :, :size] = total[:, :size].astype(bf16)
            part[c, :, size:] = parts.astype(bf16)
        else:
            part[c] = total.astype(bf16)

        @pl.loop(1, zs)
        def _(d):
            there = in_column(d)
            column_copy(
                part.at[c, t_block(there)], back2.at[c, t_block(z)], there, sc.at[c], rc.at[c]
            ).start()

        back2[c, t_block(z), :] = part[c, t_block(z), :]

    if last > 0:
        combine_and_send(0)

    sums_but = pl.ds(0, xs - 1)
    wait_e = pltpu.make_async_remote_copy(
        src_ref=sums_all.at[sums_but],
        dst_ref=sums_all.at[sums_but],
        send_sem=se,
        recv_sem=re,
        device_id={"tensor": tn},
        device_id_type=MESH,
    )
    wait_e.wait_recv()
    total = sums_all[0]
    for n in range(1, xs):
        total = total + sums_all[n]
    gap_total, ref_total = total[0:1], total[1:2]
    ratio_ref[...] = jnp.sum(gap_total, axis=1, keepdims=True) / (
        jnp.sum(ref_total, axis=1, keepdims=True) + 1e-06
    )
    high, middle, low = split3(gap_total)
    which = iota((BLOCK, rows), 0)
    stacked = jnp.where(
        which == 0, high, jnp.where(which == 1, middle, jnp.where(which == 2, low, 0.0))
    )
    size = chunks[last][1]
    out8[last, :, size:] = stacked.T.astype(bf16)
    send_back(last)

    for c in range(1, last + 1):
        combine_and_send(c)

    all_but_t = pl.ds(0, tokens - tok)
    for c, (start, size) in enumerate(chunks):
        wait_c = column_copy(part.at[c, all_but_t], back2.at[c, all_but_t], z, sc.at[c], rc.at[c])
        wait_c.wait_recv()
        total = back2[c, :tok].astype(f32)
        for n in range(1, zs):
            total = total + back2[c, n * tok : (n + 1) * tok].astype(f32)
        mixed_ref[:, start : start + size] = total[:, :size].astype(bf16)
        if c == last:
            error = jnp.sum(total[:, size:], axis=1, keepdims=True)
            diagonal = iota((tok, tok), 0) == iota((tok, tok), 1)
            token_ref[...] = jnp.sum(jnp.where(diagonal, error, 0.0), axis=0, keepdims=True)

    wait.wait_send()
    wait_g.wait_send()
    wait_2.wait_send()
    wait_x.wait_send()
    wait_e.wait_send()
    for c in range(len(chunks)):
        row_copy(
            out8.at[c, all_but_r], back1.at[c, all_but_r], r, sb.at[c], rb.at[c]
        ).wait_send()
        column_copy(
            part.at[c, all_but_t], back2.at[c, all_but_t], z, sc.at[c], rc.at[c]
        ).wait_send()


def per_device(sizes, hidden, ids, gates, code8, scale8, code4, scale4):
    zs, rs, xs, tok, top = sizes
    routes, width = tok * top, hidden.shape[2]
    rows = zs * rs * SLOTS
    inner, feats = code8.shape[1:]
    chunks = chunks_of(feats)
    count, tokens = len(chunks), zs * tok
    wide = max(chunks[-1][1] + BLOCK, chunks[0][1])
    vmem = pl.BlockSpec(memory_space=pltpu.VMEM)
    dma = pltpu.SemaphoreType.DMA
    mixed, token, ratio = pl.pallas_call(
        functools.partial(kernel, sizes),
        out_shape=(
            jax.ShapeDtypeStruct((tok, feats), bf16),
            jax.ShapeDtypeStruct((1, tok), f32),
            jax.ShapeDtypeStruct((1, 1), f32),
        ),
        in_specs=[pl.BlockSpec(memory_space=pltpu.HBM)] * 7,
        out_specs=(vmem, vmem, vmem),
        scratch_shapes=[
            pltpu.VMEM((top, tok), jnp.int32),
            pltpu.VMEM((top, tok), f32),
            pltpu.VMEM((routes, width), bf16),
            pltpu.SMEM((feats // BLOCK, 1, inner // BLOCK), f32),
            pltpu.VMEM((1, inner // BLOCK, feats), f32),
            pltpu.VMEM((inner, feats), bf16),
            pltpu.VMEM((inner, feats), bf16),
            pltpu.VMEM((rows, width), bf16),
            pltpu.VMEM((rows, BLOCK), bf16),
            pltpu.VMEM((rows, width), bf16),
            pltpu.VMEM((rows, BLOCK), bf16),
            pltpu.VMEM((rows, width), bf16),
            pltpu.VMEM((rows, xs * width), bf16),
            pltpu.VMEM((count, rows, wide), bf16),
            pltpu.VMEM((count, rows, wide), bf16),
            pltpu.VMEM((count, tokens, wide), bf16),
            pltpu.VMEM((count, tokens, wide), bf16),
            pltpu.VMEM((8, rows), f32),
            pltpu.VMEM((xs, 8, rows), f32),
            dma((5,)),
            dma((2, 2)),
        ]
        + [dma] * 10
        + [dma((count,))] * 4,
        compiler_params=pltpu.CompilerParams(
            collective_id=0, has_side_effects=True, vmem_limit_bytes=24 * 1024 * 1024
        ),
    )(
        *[
            pltpu.with_memory_space_constraint(operand, pltpu.HBM)
            for operand in (
                ids.T,
                gates.T,
                hidden.reshape(routes, width),
                jnp.transpose(scale8, (2, 0, 1)),
                scale4,
                code8,
                code4,
            )
        ]
    )
    return mixed, token.reshape(tok), ratio.reshape(1)


def solution(mesh):
    experts, xs = mesh.shape["expert"], mesh.shape["tensor"]
    zs = COLUMN
    rs = experts // zs

    def run(hidden, *rest):
        tok, top = hidden.shape[0] // experts, hidden.shape[1]
        mapped = jax.shard_map(
            functools.partial(per_device, (zs, rs, xs, tok, top)),
            mesh=mesh,
            in_specs=(
                P("expert", None, "tensor"),
                P("expert", None),
                P("expert", None),
                P("expert", None, "tensor"),
                P("expert", None, "tensor"),
                P("expert", None, "tensor"),
                P("expert", None, "tensor"),
            ),
            out_specs=(P("expert", "tensor"), P("expert"), P("expert")),
            check_vma=False,
        )
        return mapped(hidden, *rest)

    return run
```

```python
import functools

import jax
import jax.numpy as jnp
from jax import lax
from jax.experimental import pallas as pl
from jax.experimental.pallas import tpu as pltpu
from jax.sharding import PartitionSpec as P

BLOCK = 128
SLOTS = 2
SIDE = 8
CORES = 2
MESH = pl.DeviceIdType.MESH
f32, bf16 = jnp.float32, jnp.bfloat16


def iota(shape, dim):
    return lax.broadcasted_iota(jnp.int32, shape, dim)


def dot(a, b):
    return jnp.dot(a, b, preferred_element_type=f32)


def split3(value):
    high = value.astype(bf16).astype(f32)
    rest = value - high
    middle = rest.astype(bf16).astype(f32)
    return high, middle, rest - middle


def chunks_of(width):
    full = 2 * BLOCK
    pieces = [(s, min(full, width - s)) for s in range(0, width, full)]
    chunks = [(1 - n % 2, start, size) for n, (start, size) in enumerate(pieces)]
    return chunks + [(0, width, BLOCK)]


class Path:
    def __init__(self, number, me):
        rest = lax.rem(me, SIDE * CORES)
        z, y, core = me // (SIDE * CORES), rest // CORES, lax.rem(rest, CORES)
        self.number, self.core = number, core
        self.place, self.other = (z, y) if number == 0 else (y, z)
        self.spot = self.other * CORES + core

    def column(self, there):
        if self.number == 0:
            return there * (SIDE * CORES) + self.spot
        return self.other * (SIDE * CORES) + there * CORES + self.core

    def row(self, there):
        if self.number == 0:
            return self.place * (SIDE * CORES) + there
        return there // CORES * (SIDE * CORES) + self.place * CORES + lax.rem(there, CORES)


def far_first(d, count):
    step = d // 2
    return count // 2 + jnp.where(d % 2 == 1, -step, step)


def kernel(
    sizes,
    ids_hbm, gate_hbm, hidden_hbm, scale8_hbm, scale4_hbm, code8_hbm, code4_hbm,
    mixed_ref, token_ref, ratio_ref,
    ids_ref, gate_ref, hidden_ref, scale8_ref, scale4_ref, w8, w4, send1, gates1, recv1, grecv,
    send2, x_all, x_turned, sums, sums_all, outs, backs, parts, ends,
    small_sem, code_sem, s1, r1, sg, rg, s2, r2, sx, rx, se, re, sb, rb, sc, rc,
):
    xs, tok, top = sizes
    routes = tok * top
    spots = SIDE * CORES
    rows = SIDE * spots * SLOTS
    c_rows, r_rows = spots * SLOTS, SIDE * SLOTS
    tokens = SIDE * tok
    width = hidden_ref.shape[1]
    inner, feats = w8.shape
    chunks = chunks_of(feats)
    last = len(chunks) - 1

    me, tn = lax.axis_index("expert"), lax.axis_index("tensor")
    paths = Path(0, me), Path(1, me)
    first = paths[0]

    def in_column(path, d):
        return lax.rem(path.place + far_first(d, SIDE), SIDE)

    def in_row(path, d):
        return lax.rem(path.spot + far_first(d, spots), spots)

    def in_gather(d):
        return lax.rem(tn + d, xs)

    small = (
        (ids_hbm, ids_ref),
        (gate_hbm, gate_ref),
        (hidden_hbm, hidden_ref),
        (scale8_hbm, scale8_ref),
        (scale4_hbm, scale4_ref),
    )
    small_copies = []
    for n, (src, dst) in enumerate(small):
        copy = pltpu.make_async_copy(src, dst, small_sem.at[n])
        copy.start()
        small_copies.append(copy)

    barrier = pltpu.get_barrier_semaphore()

    def signal(device):
        pl.semaphore_signal(barrier, inc=1, device_id=device, device_id_type=MESH)

    @pl.loop(1, SIDE)
    def _(d):
        for path in paths:
            step = in_column(path, d) * CORES
            for core in range(CORES):
                signal({"expert": paths[1 - path.number].row(step + core)})

    signal({"expert": first.row(first.other * CORES + 1 - first.core)})

    @pl.loop(1, xs)
    def _(d):
        signal({"tensor": in_gather(d)})

    part_rows = inner // 2
    code_copies = []
    for n, (src, dst) in enumerate(((code8_hbm, w8), (code4_hbm, w4))):
        for h in range(2):
            piece = pl.ds(h * part_rows, part_rows)
            copy = pltpu.make_async_copy(src.at[0, piece, :], dst.at[piece, :], code_sem.at[n, h])
            copy.start()
            code_copies.append(copy)

    for copy in small_copies[:3]:
        copy.wait()
    gate = gate_ref[...]
    high = gate.astype(bf16).astype(f32)
    table = jnp.concatenate([ids_ref[...].astype(f32), high, gate - high], axis=0).astype(bf16)
    repeat = (iota((tok, routes), 0) == iota((tok, routes), 1) // top).astype(f32).astype(bf16)
    table = dot(table, repeat)
    own_choice = iota((top, routes), 0) == iota((top, routes), 1) % top

    def flat(n):
        rows_of = table[n * top : (n + 1) * top]
        return jnp.sum(jnp.where(own_choice, rows_of, 0.0), axis=0, keepdims=True)

    flat_ids, gate_high, gate_low = flat(0), flat(1), flat(2)
    ids = jnp.broadcast_to(flat_ids, (routes, routes))
    earlier = (ids == ids.T) & (iota((routes, routes), 0) < iota((routes, routes), 1))
    position = jnp.sum(jnp.where(earlier, 1.0, 0.0), axis=0, keepdims=True).astype(jnp.int32)
    expert = flat_ids.astype(jnp.int32)
    target = expert % spots * r_rows + expert // spots * SLOTS + position
    chosen = iota((rows, routes), 0) == target
    send1[...] = dot(chosen.astype(f32).astype(bf16), hidden_ref[...]).astype(bf16)

    pl.semaphore_wait(barrier, 2 * (SIDE - 1) + spots - 1 + xs - 1)

    def copy_to(device, src, dst, send, recv):
        return pltpu.make_async_remote_copy(
            src_ref=src,
            dst_ref=dst,
            send_sem=send,
            recv_sem=recv,
            device_id=device,
            device_id_type=MESH,
        )

    here = {"expert": me}

    def c_block(n):
        return pl.ds(pl.multiple_of(n * c_rows, c_rows), c_rows)

    def r_block(n):
        return pl.ds(pl.multiple_of(n * r_rows, r_rows), r_rows)

    def t_block(n):
        return pl.ds(pl.multiple_of(n * tok, tok), tok)

    def row_exchange(path, src, dst, send, recv):
        @pl.loop(1, spots)
        def _(d):
            there = in_row(path, d)
            copy_to(
                {"expert": path.row(there)},
                src.at[r_block(there)],
                dst.at[r_block(path.spot)],
                send,
                recv,
            ).start()

    def column_exchange(path, src, dst, send, recv):
        @pl.loop(1, SIDE)
        def _(d):
            there = in_column(path, d)
            copy_to(
                {"expert": path.column(there)},
                src.at[c_block(there)],
                dst.at[c_block(path.place)],
                send,
                recv,
            ).start()

    row_exchange(first, send1, recv1, s1, r1)
    recv1[r_block(first.spot), :] = send1[r_block(first.spot), :]

    lanes = gates1.shape[2]
    token_of = iota((routes, lanes), 0) // top
    lane = iota((routes, lanes), 1)
    spread_high = (lane == token_of).astype(f32).astype(bf16)
    spread_low = (lane == token_of + tok).astype(f32).astype(bf16)
    turned = expert // CORES % SIDE * c_rows + expert // spots * CORES * SLOTS
    turned = turned + expert % CORES * SLOTS + position
    for path, target in zip(paths, (expert * SLOTS + position, turned)):
        chosen = iota((rows, routes), 0) == target
        gates = dot(jnp.where(chosen, gate_high, 0.0).astype(bf16), spread_high)
        gates = gates + dot(jnp.where(chosen, gate_low, 0.0).astype(bf16), spread_low)
        gates1[path.number] = gates.astype(bf16)

    def scale_weights(begin, end):
        @pl.loop(begin, end)
        def _(g):
            group = pl.ds(pl.multiple_of(g * BLOCK, BLOCK), BLOCK)
            for b in range(feats // BLOCK):
                cols = pl.ds(b * BLOCK, BLOCK)
                w8[group, cols] = (w8[group, cols].astype(f32) * scale8_ref[b, 0, g]).astype(bf16)
            w4[group, :] = (w4[group, :].astype(f32) * scale4_ref[0, pl.ds(g, 1), :]).astype(bf16)

    groups = inner // BLOCK
    for copy in small_copies[3:] + code_copies:
        copy.wait()
    scale_weights(0, groups // 4)

    at, of = iota((rows, rows), 0), iota((rows, rows), 1)
    low_place, slot = at % r_rows // SLOTS, at % SLOTS
    reorder = of == low_place * c_rows + at // r_rows * SLOTS + slot
    reorder = reorder.astype(f32).astype(bf16)
    turn = of == low_place * c_rows + at % c_rows // r_rows * r_rows + at // c_rows * SLOTS + slot
    turn = turn.astype(f32).astype(bf16)

    but_c, but_r = pl.ds(0, rows - c_rows), pl.ds(0, rows - r_rows)
    wait_1 = copy_to(here, send1.at[but_r], recv1.at[but_r], s1, r1)
    wait_1.wait_recv()
    send2[...] = dot(turn, recv1[...]).astype(bf16)

    mine = pl.ds(pl.multiple_of(tn * width, width), width)
    arrived = x_all.at[:, mine]
    column_exchange(first, send2, arrived, s2, r2.at[first.place])
    x_all[c_block(first.place), mine] = send2[c_block(first.place), :]
    for path in paths:
        n = path.number
        column_exchange(path, gates1.at[n], grecv.at[n], sg.at[n], rg.at[n])
        grecv[n, c_block(path.place), :] = gates1[n, c_block(path.place), :]

    scale_weights(groups // 4, groups // 2)

    for n in range(SIDE):
        step = n // 2 if n % 2 == 0 else -(n // 2 + 1)
        source = lax.rem(first.place + SIDE + step, SIDE)
        block = c_block(source)
        if n > 0:
            copy_to(here, send2.at[block], arrived.at[block], s2, r2.at[source]).wait_recv()

        @pl.loop(1, xs)
        def _(d):
            copy_to(
                {"tensor": in_gather(d)}, arrived.at[block], arrived.at[block], sx, rx
            ).start()

    wait_2 = copy_to(here, send2.at[but_c], arrived.at[but_c], s2, r2.at[0])

    place, wide = iota((lanes, 2 * tokens), 0), iota((lanes, 2 * tokens), 1)
    widen = (place == wide % tok + jnp.where(wide < tokens, 0, tok)).astype(f32).astype(bf16)
    row_place = iota((rows, 2 * tokens), 0) % r_rows // SLOTS
    own_place = row_place == iota((rows, 2 * tokens), 1) % tokens // tok
    combine, waits_g = [], []
    for path in paths:
        n = path.number
        wait_g = copy_to(here, gates1.at[n, but_c], grecv.at[n, but_c], sg.at[n], rg.at[n])
        wait_g.wait_recv()
        waits_g.append(wait_g)
        gates = dot(dot(reorder, grecv[n]).astype(bf16), widen)
        combine.append(jnp.where(own_place, gates, 0.0).T.astype(bf16))

    scale_weights(groups // 2, groups)
    others = pl.ds(0, (xs - 1) * width)
    wait_x = copy_to(here, x_all.at[:, others], x_all.at[:, others], sx, rx)
    wait_x.wait_recv()

    def send_back(c):
        path = paths[chunks[c][0]]

        @pl.loop(1, spots)
        def _(d):
            there = in_row(path, d)
            copy_to(
                {"expert": path.row(there)},
                outs[c].at[r_block(there)],
                backs[c].at[r_block(path.spot)],
                sb.at[c],
                rb.at[c],
            ).start()

        backs[c][r_block(path.spot), :] = outs[c][r_block(path.spot), :]

    early = min(2, last)
    for c, (number, start, size) in enumerate(chunks[:last]):
        if c == 1:
            x_turned[...] = dot(turn, x_all[...]).astype(bf16)
        activation = x_all if number else x_turned
        outs[c][...] = dot(activation[...], w8[:, start : start + size]).astype(bf16)
        if c < early:
            send_back(c)
    gap_sums = [jnp.zeros((rows, BLOCK), f32), jnp.zeros((rows, BLOCK), f32)]
    ref_sum = jnp.zeros((rows, BLOCK), f32)
    for c, (number, start, size) in enumerate(chunks[:last]):
        activation = x_all if number else x_turned
        result4 = dot(activation[...], w4[:, start : start + size]).astype(bf16).astype(f32)
        result8 = outs[c][...].astype(f32)
        gap = result4 - result8
        for b in range(size // BLOCK):
            cols = slice(b * BLOCK, (b + 1) * BLOCK)
            gap_sums[number] += gap[:, cols] * gap[:, cols]
            ref_sum += result8[:, cols] * result8[:, cols]

    def stack3(value, count):
        high, middle, low = split3(value)
        which = iota((count, rows), 0)
        low = jnp.where(which == 2, low, 0.0)
        return jnp.where(which == 0, high, jnp.where(which == 1, middle, low)).astype(bf16)

    gap_rows = [jnp.sum(gap_sum.T, axis=0, keepdims=True) for gap_sum in gap_sums]
    moved = jnp.sum(dot(stack3(gap_rows[1], 8), turn), axis=0, keepdims=True)
    gap_row = gap_rows[0] + moved
    outs[last][...] = stack3(gap_row, BLOCK).astype(f32).T.astype(bf16)
    for c in [last] + list(range(early, last)):
        send_back(c)
    gap_part = jnp.sum(gap_row, axis=1, keepdims=True)
    ref_part = jnp.sum(jnp.sum(ref_sum, axis=0, keepdims=True), axis=1, keepdims=True)

    def wait_back(c):
        return copy_to(here, outs[c].at[but_r], backs[c].at[but_r], sb.at[c], rb.at[c])

    def wait_end(c):
        some = pl.ds(0, SIDE - 1) if c == last else pl.ds(0, tokens - tok)
        return copy_to(here, ends[c].at[some], ends[c].at[some], sc.at[c], rc.at[c])

    def combine_and_send(c):
        path = paths[chunks[c][0]]
        wait_back(c).wait_recv()
        both = dot(combine[path.number], backs[c][...])
        total = both[:tokens] + both[tokens:]
        if c == last:
            error = jnp.sum(total, axis=1, keepdims=True)
            parts[c][...] = jnp.broadcast_to(error, (tokens, BLOCK)).T[:8]
        else:
            parts[c][...] = total.astype(bf16)

        @pl.loop(1, SIDE)
        def _(d):
            there = in_column(path, d)
            copy_to(
                {"expert": path.column(there)},
                parts[c] if c == last else parts[c].at[t_block(there)],
                ends[c].at[path.place] if c == last else ends[c].at[t_block(path.place)],
                sc.at[c],
                rc.at[c],
            ).start()

        if c == last:
            ends[c][path.place] = parts[c][...]
        else:
            ends[c][t_block(path.place), :] = parts[c][t_block(path.place), :]

    order = list(range(early)) + [last] + list(range(early, last))
    for c in order:
        combine_and_send(c)

    for c in order:
        wait_end(c).wait_recv()
        if c < last:
            _, start, size = chunks[c]
            total = ends[c][:tok].astype(f32)
            for n in range(1, SIDE):
                total = total + ends[c][n * tok : (n + 1) * tok].astype(f32)
            mixed_ref[:, start : start + size] = total.astype(bf16)
        else:
            total = ends[c][0]
            for n in range(1, SIDE):
                total = total + ends[c][n]
            which = iota((8, tokens), 0)
            sums[...] = jnp.where(which == 0, total, jnp.where(which == 1, gap_part, ref_part))
            sums_all[tn] = sums[...]

            @pl.loop(1, xs)
            def _(d):
                copy_to({"tensor": in_gather(d)}, sums, sums_all.at[tn], se, re).start()

    sums_but = pl.ds(0, xs - 1)
    wait_e = copy_to(here, sums_all.at[sums_but], sums_all.at[sums_but], se, re)
    wait_e.wait_recv()
    total = sums_all[0]
    for n in range(1, xs):
        total = total + sums_all[n]
    ratio_ref[...] = total[1:2, :1] / (total[2:3, :1] + 1e-06)
    place = iota((tok, tokens), 1) - paths[chunks[last][0]].place * tok
    error = jnp.where(place == iota((tok, tokens), 0), total[0:1], 0.0)
    error = jnp.sum(error, axis=1, keepdims=True)
    diagonal = iota((tok, tok), 0) == iota((tok, tok), 1)
    token_ref[...] = jnp.sum(jnp.where(diagonal, error, 0.0), axis=0, keepdims=True)

    for wait in [wait_1, wait_2, wait_x, wait_e] + waits_g:
        wait.wait_send()
    for c in range(last + 1):
        wait_back(c).wait_send()
        wait_end(c).wait_send()


def per_device(sizes, hidden, ids, gates, code8, scale8, code4, scale4):
    xs, tok, top = sizes
    routes, width = tok * top, hidden.shape[2]
    rows = SIDE * SIDE * CORES * SLOTS
    inner, feats = code8.shape[1:]
    chunks = chunks_of(feats)
    count, tokens = len(chunks), SIDE * tok
    vmem = pl.BlockSpec(memory_space=pltpu.VMEM)
    dma = pltpu.SemaphoreType.DMA
    mixed, token, ratio = pl.pallas_call(
        functools.partial(kernel, sizes),
        out_shape=(
            jax.ShapeDtypeStruct((tok, feats), bf16),
            jax.ShapeDtypeStruct((1, tok), f32),
            jax.ShapeDtypeStruct((1, 1), f32),
        ),
        in_specs=[pl.BlockSpec(memory_space=pltpu.HBM)] * 7,
        out_specs=(vmem, vmem, vmem),
        scratch_shapes=[
            pltpu.VMEM((top, tok), jnp.int32),
            pltpu.VMEM((top, tok), f32),
            pltpu.VMEM((routes, width), bf16),
            pltpu.SMEM((feats // BLOCK, 1, inner // BLOCK), f32),
            pltpu.VMEM((1, inner // BLOCK, feats), f32),
            pltpu.VMEM((inner, feats), bf16),
            pltpu.VMEM((inner, feats), bf16),
            pltpu.VMEM((rows, width), bf16),
            pltpu.VMEM((2, rows, BLOCK), bf16),
            pltpu.VMEM((rows, width), bf16),
            pltpu.VMEM((2, rows, BLOCK), bf16),
            pltpu.VMEM((rows, width), bf16),
            pltpu.VMEM((rows, xs * width), bf16),
            pltpu.VMEM((rows, xs * width), bf16),
            pltpu.VMEM((8, tokens), f32),
            pltpu.VMEM((xs, 8, tokens), f32),
            [pltpu.VMEM((rows, size), bf16) for _, _, size in chunks],
            [pltpu.VMEM((rows, size), bf16) for _, _, size in chunks],
            [pltpu.VMEM((tokens, size), bf16) for _, _, size in chunks[:-1]]
            + [pltpu.VMEM((8, tokens), f32)],
            [pltpu.VMEM((tokens, size), bf16) for _, _, size in chunks[:-1]]
            + [pltpu.VMEM((SIDE, 8, tokens), f32)],
            dma((5,)),
            dma((2, 2)),
            dma,
            dma,
            dma((2,)),
            dma((2,)),
            dma,
            dma((SIDE,)),
        ]
        + [dma] * 4
        + [dma((count,))] * 4,
        compiler_params=pltpu.CompilerParams(
            collective_id=0, has_side_effects=True, vmem_limit_bytes=24 * 1024 * 1024
        ),
    )(
        *[
            pltpu.with_memory_space_constraint(operand, pltpu.HBM)
            for operand in (
                ids.T,
                gates.T,
                hidden.reshape(routes, width),
                jnp.transpose(scale8, (2, 0, 1)),
                scale4,
                code8,
                code4,
            )
        ]
    )
    return mixed, token.reshape(tok), ratio.reshape(1)


def solution(mesh):
    experts, xs = mesh.shape["expert"], mesh.shape["tensor"]
    assert experts == SIDE * SIDE * CORES

    def run(hidden, *rest):
        tok, top = hidden.shape[0] // experts, hidden.shape[1]
        mapped = jax.shard_map(
            functools.partial(per_device, (xs, tok, top)),
            mesh=mesh,
            in_specs=(
                P("expert", None, "tensor"),
                P("expert", None),
                P("expert", None),
                P("expert", None, "tensor"),
                P("expert", None, "tensor"),
                P("expert", None, "tensor"),
                P("expert", None, "tensor"),
            ),
            out_specs=(P("expert", "tensor"), P("expert"), P("expert")),
            check_vma=False,
        )
        return mapped(hidden, *rest)

    return run
```

```python
import functools

import jax
import jax.numpy as jnp
from jax import lax
from jax.experimental import pallas as pl
from jax.experimental.pallas import tpu as pltpu
from jax.sharding import PartitionSpec as P

BLOCK = 128
SLOTS = 2
SIDE = 8
CORES = 2
EARLY = 2
MESH = pl.DeviceIdType.MESH
f32, bf16 = jnp.float32, jnp.bfloat16


def iota(shape, dim):
    return lax.broadcasted_iota(jnp.int32, shape, dim)


def dot(a, b):
    return jnp.dot(a, b, preferred_element_type=f32)


def split3(value):
    high = value.astype(bf16).astype(f32)
    rest = value - high
    middle = rest.astype(bf16).astype(f32)
    return high, middle, rest - middle


def chunks_of(width):
    full = 2 * BLOCK
    starts = [0] + list(range(width % full or full, width, full))
    ends = starts[1:] + [width]
    chunks = [(1 - n % 2, a, b - a) for n, (a, b) in enumerate(zip(starts, ends))]
    return chunks + [(1, width, BLOCK)]


class Path:
    def __init__(self, number, me):
        rest = lax.rem(me, SIDE * CORES)
        z, y, core = me // (SIDE * CORES), rest // CORES, lax.rem(rest, CORES)
        self.number, self.core = number, core
        self.place, self.other = (z, y) if number == 0 else (y, z)
        self.spot = self.other * CORES + core

    def column(self, there):
        if self.number == 0:
            return there * (SIDE * CORES) + self.spot
        return self.other * (SIDE * CORES) + there * CORES + self.core

    def row(self, there):
        if self.number == 0:
            return self.place * (SIDE * CORES) + there
        return there // CORES * (SIDE * CORES) + self.place * CORES + lax.rem(there, CORES)


def far_first(d, count):
    step = d // 2
    return count // 2 + jnp.where(d % 2 == 1, -step, step)


def kernel(
    sizes,
    ids_hbm, gate_hbm, hidden_hbm, scale8_hbm, scale4_hbm, code8_hbm, code4_hbm,
    mixed_ref, token_ref, ratio_ref,
    ids_ref, gate_ref, hidden_ref, scale8_ref, scale4_ref, w8, w4, send1, gates1, recv1, grecv,
    send2, x_all, x_turned, sums, sums_all, outs, backs, parts, ends,
    small_sem, code_sem, s1, r1, sg, rg, s2, r2, sx, rx, se, re, sb, rb, sc, rc,
):
    xs, tok, top = sizes
    routes = tok * top
    spots = SIDE * CORES
    rows = SIDE * spots * SLOTS
    c_rows, r_rows = spots * SLOTS, SIDE * SLOTS
    tokens = SIDE * tok
    width = hidden_ref.shape[1]
    inner, feats = w8.shape
    chunks = chunks_of(feats)
    last = len(chunks) - 1

    me, tn = lax.axis_index("expert"), lax.axis_index("tensor")
    paths = Path(0, me), Path(1, me)
    first = paths[0]

    def in_column(path, d):
        return lax.rem(path.place + far_first(d, SIDE), SIDE)

    def in_row(path, d):
        return lax.rem(path.spot + far_first(d, spots), spots)

    def in_gather(d):
        return lax.rem(tn + d, xs)

    barrier = pltpu.get_barrier_semaphore()

    def signal(device):
        pl.semaphore_signal(barrier, inc=1, device_id=device, device_id_type=MESH)

    @pl.loop(1, SIDE)
    def _(d):
        for path in paths:
            step = in_column(path, d) * CORES
            for core in range(CORES):
                signal({"expert": paths[1 - path.number].row(step + core)})

    signal({"expert": first.row(first.other * CORES + 1 - first.core)})

    @pl.loop(1, xs)
    def _(d):
        signal({"tensor": in_gather(d)})

    small = (
        (ids_hbm, ids_ref),
        (gate_hbm, gate_ref),
        (hidden_hbm, hidden_ref),
        (scale8_hbm, scale8_ref),
        (scale4_hbm, scale4_ref),
    )
    small_copies = []
    for n, (src, dst) in enumerate(small):
        copy = pltpu.make_async_copy(src, dst, small_sem.at[n])
        copy.start()
        small_copies.append(copy)
    part_rows = inner // 2
    code_copies = []
    for n, (src, dst) in enumerate(((code8_hbm, w8), (code4_hbm, w4))):
        for h in range(2):
            piece = pl.ds(h * part_rows, part_rows)
            copy = pltpu.make_async_copy(src.at[0, piece, :], dst.at[piece, :], code_sem.at[n, h])
            copy.start()
            code_copies.append(copy)

    for copy in small_copies[:3]:
        copy.wait()
    gate = gate_ref[...]
    high = gate.astype(bf16).astype(f32)
    table = jnp.concatenate([ids_ref[...].astype(f32), high, gate - high], axis=0).astype(bf16)
    repeat = (iota((tok, routes), 0) == iota((tok, routes), 1) // top).astype(f32).astype(bf16)
    table = dot(table, repeat)
    own_choice = iota((top, routes), 0) == iota((top, routes), 1) % top

    def flat(n):
        rows_of = table[n * top : (n + 1) * top]
        return jnp.sum(jnp.where(own_choice, rows_of, 0.0), axis=0, keepdims=True)

    flat_ids, gate_high, gate_low = flat(0), flat(1), flat(2)
    ids = jnp.broadcast_to(flat_ids, (routes, routes))
    earlier = (ids == ids.T) & (iota((routes, routes), 0) < iota((routes, routes), 1))
    position = jnp.sum(jnp.where(earlier, 1.0, 0.0), axis=0, keepdims=True).astype(jnp.int32)
    expert = flat_ids.astype(jnp.int32)
    target = expert % spots * r_rows + expert // spots * SLOTS + position
    chosen = iota((rows, routes), 0) == target
    send1[...] = dot(chosen.astype(f32).astype(bf16), hidden_ref[...]).astype(bf16)

    pl.semaphore_wait(barrier, 2 * (SIDE - 1) + spots - 1 + xs - 1)

    def copy_to(device, src, dst, send, recv):
        return pltpu.make_async_remote_copy(
            src_ref=src,
            dst_ref=dst,
            send_sem=send,
            recv_sem=recv,
            device_id=device,
            device_id_type=MESH,
        )

    here = {"expert": me}

    def c_block(n):
        return pl.ds(pl.multiple_of(n * c_rows, c_rows), c_rows)

    def r_block(n):
        return pl.ds(pl.multiple_of(n * r_rows, r_rows), r_rows)

    def t_block(n):
        return pl.ds(pl.multiple_of(n * tok, tok), tok)

    def row_exchange(path, src, dst, send, recv):
        @pl.loop(1, spots)
        def _(d):
            there = in_row(path, d)
            copy_to(
                {"expert": path.row(there)},
                src.at[r_block(there)],
                dst.at[r_block(path.spot)],
                send,
                recv,
            ).start()

    def column_exchange(path, src, dst, send, recv):
        @pl.loop(1, SIDE)
        def _(d):
            there = in_column(path, d)
            copy_to(
                {"expert": path.column(there)},
                src.at[c_block(there)],
                dst.at[c_block(path.place)],
                send,
                recv,
            ).start()

    row_exchange(first, send1, recv1, s1, r1)
    recv1[r_block(first.spot), :] = send1[r_block(first.spot), :]

    lanes = gates1.shape[2]
    token_of = iota((routes, lanes), 0) // top
    lane = iota((routes, lanes), 1)
    spread_high = (lane == token_of).astype(f32).astype(bf16)
    spread_low = (lane == token_of + tok).astype(f32).astype(bf16)
    turned = expert // CORES % SIDE * c_rows + expert // spots * CORES * SLOTS
    turned = turned + expert % CORES * SLOTS + position
    for path, target in zip(paths, (expert * SLOTS + position, turned)):
        chosen = iota((rows, routes), 0) == target
        gates = dot(jnp.where(chosen, gate_high, 0.0).astype(bf16), spread_high)
        gates = gates + dot(jnp.where(chosen, gate_low, 0.0).astype(bf16), spread_low)
        gates1[path.number] = gates.astype(bf16)

    def scale_weights(begin, end):
        @pl.loop(begin, end)
        def _(g):
            group = pl.ds(pl.multiple_of(g * BLOCK, BLOCK), BLOCK)
            for b in range(feats // BLOCK):
                cols = pl.ds(b * BLOCK, BLOCK)
                w8[group, cols] = (w8[group, cols].astype(f32) * scale8_ref[b, 0, g]).astype(bf16)
            w4[group, :] = (w4[group, :].astype(f32) * scale4_ref[0, pl.ds(g, 1), :]).astype(bf16)

    groups = inner // BLOCK
    for copy in small_copies[3:] + code_copies:
        copy.wait()
    scale_weights(0, groups // 4)

    at, of = iota((rows, rows), 0), iota((rows, rows), 1)
    low_place, slot = at % r_rows // SLOTS, at % SLOTS
    reorder = of == low_place * c_rows + at // r_rows * SLOTS + slot
    reorder = reorder.astype(f32).astype(bf16)
    turn = of == low_place * c_rows + at % c_rows // r_rows * r_rows + at // c_rows * SLOTS + slot
    turn = turn.astype(f32).astype(bf16)

    but_c, but_r = pl.ds(0, rows - c_rows), pl.ds(0, rows - r_rows)
    wait_1 = copy_to(here, send1.at[but_r], recv1.at[but_r], s1, r1)
    wait_1.wait_recv()
    send2[...] = dot(turn, recv1[...]).astype(bf16)

    mine = pl.ds(pl.multiple_of(tn * width, width), width)
    arrived = x_all.at[:, mine]
    column_exchange(first, send2, arrived, s2, r2.at[first.place])
    x_all[c_block(first.place), mine] = send2[c_block(first.place), :]
    for path in paths:
        n = path.number
        column_exchange(path, gates1.at[n], grecv.at[n], sg.at[n], rg.at[n])
        grecv[n, c_block(path.place), :] = gates1[n, c_block(path.place), :]

    scale_weights(groups // 4, groups // 2)

    for n in range(SIDE):
        step = n // 2 if n % 2 == 0 else -(n // 2 + 1)
        source = lax.rem(first.place + SIDE + step, SIDE)
        block = c_block(source)
        if n > 0:
            copy_to(here, send2.at[block], arrived.at[block], s2, r2.at[source]).wait_recv()

        @pl.loop(1, xs)
        def _(d):
            copy_to(
                {"tensor": in_gather(d)}, arrived.at[block], arrived.at[block], sx, rx
            ).start()

    wait_2 = copy_to(here, send2.at[but_c], arrived.at[but_c], s2, r2.at[0])

    place, wide = iota((lanes, 2 * tokens), 0), iota((lanes, 2 * tokens), 1)
    widen = (place == wide % tok + jnp.where(wide < tokens, 0, tok)).astype(f32).astype(bf16)
    row_place = iota((rows, 2 * tokens), 0) % r_rows // SLOTS
    own_place = row_place == iota((rows, 2 * tokens), 1) % tokens // tok
    combine, waits_g = [], []
    for path in paths:
        n = path.number
        wait_g = copy_to(here, gates1.at[n, but_c], grecv.at[n, but_c], sg.at[n], rg.at[n])
        wait_g.wait_recv()
        waits_g.append(wait_g)
        gates = dot(dot(reorder, grecv[n]).astype(bf16), widen)
        combine.append(jnp.where(own_place, gates, 0.0).T.astype(bf16))

    scale_weights(groups // 2, groups)
    others = pl.ds(0, (xs - 1) * width)
    wait_x = copy_to(here, x_all.at[:, others], x_all.at[:, others], sx, rx)
    wait_x.wait_recv()

    def send_back(c):
        path = paths[chunks[c][0]]

        @pl.loop(1, spots)
        def _(d):
            there = in_row(path, d)
            copy_to(
                {"expert": path.row(there)},
                outs[c].at[r_block(there)],
                backs[c].at[r_block(path.spot)],
                sb.at[c],
                rb.at[c],
            ).start()

        backs[c][r_block(path.spot), :] = outs[c][r_block(path.spot), :]

    early = min(EARLY, last)
    for c, (number, start, size) in enumerate(chunks[:last]):
        if c == 1:
            x_turned[...] = dot(turn, x_all[...]).astype(bf16)
        activation = x_all if number else x_turned
        outs[c][...] = dot(activation[...], w8[:, start : start + size]).astype(bf16)
        if c < early:
            send_back(c)
    gap_sums = [jnp.zeros((rows, BLOCK), f32), jnp.zeros((rows, BLOCK), f32)]
    ref_sum = jnp.zeros((rows, BLOCK), f32)
    for c, (number, start, size) in enumerate(chunks[:last]):
        activation = x_all if number else x_turned
        result4 = dot(activation[...], w4[:, start : start + size]).astype(bf16).astype(f32)
        result8 = outs[c][...].astype(f32)
        gap = result4 - result8
        for b in range(size // BLOCK):
            cols = slice(b * BLOCK, (b + 1) * BLOCK)
            gap_sums[number] += gap[:, cols] * gap[:, cols]
            ref_sum += result8[:, cols] * result8[:, cols]

    def stack3(value, count):
        high, middle, low = split3(value)
        which = iota((count, rows), 0)
        low = jnp.where(which == 2, low, 0.0)
        return jnp.where(which == 0, high, jnp.where(which == 1, middle, low)).astype(bf16)

    gap_rows = [jnp.sum(gap_sum.T, axis=0, keepdims=True) for gap_sum in gap_sums]
    last_path = chunks[last][0]
    moved = jnp.sum(dot(stack3(gap_rows[1 - last_path], 8), turn), axis=0, keepdims=True)
    gap_row = gap_rows[last_path] + moved
    outs[last][...] = stack3(gap_row, BLOCK).astype(f32).T.astype(bf16)
    for c in [last] + list(range(early, last)):
        send_back(c)
    gap_part = jnp.sum(gap_row, axis=1, keepdims=True)
    ref_part = jnp.sum(jnp.sum(ref_sum, axis=0, keepdims=True), axis=1, keepdims=True)

    def wait_back(c):
        return copy_to(here, outs[c].at[but_r], backs[c].at[but_r], sb.at[c], rb.at[c])

    def wait_end(c):
        some = pl.ds(0, SIDE - 1) if c == last else pl.ds(0, tokens - tok)
        return copy_to(here, ends[c].at[some], ends[c].at[some], sc.at[c], rc.at[c])

    def combine_and_send(c):
        path = paths[chunks[c][0]]
        wait_back(c).wait_recv()
        both = dot(combine[path.number], backs[c][...])
        total = both[:tokens] + both[tokens:]
        if c == last:
            error = jnp.sum(total, axis=1, keepdims=True)
            parts[c][...] = jnp.broadcast_to(error, (tokens, BLOCK)).T[:8]
        else:
            parts[c][...] = total.astype(bf16)

        @pl.loop(1, SIDE)
        def _(d):
            there = in_column(path, d)
            copy_to(
                {"expert": path.column(there)},
                parts[c] if c == last else parts[c].at[t_block(there)],
                ends[c].at[path.place] if c == last else ends[c].at[t_block(path.place)],
                sc.at[c],
                rc.at[c],
            ).start()

        if c == last:
            ends[c][path.place] = parts[c][...]
        else:
            ends[c][t_block(path.place), :] = parts[c][t_block(path.place), :]

    order = list(range(early)) + [last] + list(range(early, last))
    for c in order:
        combine_and_send(c)

    for c in order:
        wait_end(c).wait_recv()
        if c < last:
            _, start, size = chunks[c]
            total = ends[c][:tok].astype(f32)
            for n in range(1, SIDE):
                total = total + ends[c][n * tok : (n + 1) * tok].astype(f32)
            mixed_ref[:, start : start + size] = total.astype(bf16)
        else:
            total = ends[c][0]
            for n in range(1, SIDE):
                total = total + ends[c][n]
            which = iota((8, tokens), 0)
            sums[...] = jnp.where(which == 0, total, jnp.where(which == 1, gap_part, ref_part))
            sums_all[tn] = sums[...]

            @pl.loop(1, xs)
            def _(d):
                copy_to({"tensor": in_gather(d)}, sums, sums_all.at[tn], se, re).start()

    sums_but = pl.ds(0, xs - 1)
    wait_e = copy_to(here, sums_all.at[sums_but], sums_all.at[sums_but], se, re)
    wait_e.wait_recv()
    total = sums_all[0]
    for n in range(1, xs):
        total = total + sums_all[n]
    ratio_ref[...] = total[1:2, :1] / (total[2:3, :1] + 1e-06)
    place = iota((tok, tokens), 1) - paths[chunks[last][0]].place * tok
    error = jnp.where(place == iota((tok, tokens), 0), total[0:1], 0.0)
    error = jnp.sum(error, axis=1, keepdims=True)
    diagonal = iota((tok, tok), 0) == iota((tok, tok), 1)
    token_ref[...] = jnp.sum(jnp.where(diagonal, error, 0.0), axis=0, keepdims=True)

    for wait in [wait_1, wait_2, wait_x, wait_e] + waits_g:
        wait.wait_send()
    for c in range(last + 1):
        wait_back(c).wait_send()
        wait_end(c).wait_send()


def per_device(sizes, hidden, ids, gates, code8, scale8, code4, scale4):
    xs, tok, top = sizes
    routes, width = tok * top, hidden.shape[2]
    rows = SIDE * SIDE * CORES * SLOTS
    inner, feats = code8.shape[1:]
    chunks = chunks_of(feats)
    count, tokens = len(chunks), SIDE * tok
    vmem = pl.BlockSpec(memory_space=pltpu.VMEM)
    dma = pltpu.SemaphoreType.DMA
    mixed, token, ratio = pl.pallas_call(
        functools.partial(kernel, sizes),
        out_shape=(
            jax.ShapeDtypeStruct((tok, feats), bf16),
            jax.ShapeDtypeStruct((1, tok), f32),
            jax.ShapeDtypeStruct((1, 1), f32),
        ),
        in_specs=[pl.BlockSpec(memory_space=pltpu.HBM)] * 7,
        out_specs=(vmem, vmem, vmem),
        scratch_shapes=[
            pltpu.VMEM((top, tok), jnp.int32),
            pltpu.VMEM((top, tok), f32),
            pltpu.VMEM((routes, width), bf16),
            pltpu.SMEM((feats // BLOCK, 1, inner // BLOCK), f32),
            pltpu.VMEM((1, inner // BLOCK, feats), f32),
            pltpu.VMEM((inner, feats), bf16),
            pltpu.VMEM((inner, feats), bf16),
            pltpu.VMEM((rows, width), bf16),
            pltpu.VMEM((2, rows, BLOCK), bf16),
            pltpu.VMEM((rows, width), bf16),
            pltpu.VMEM((2, rows, BLOCK), bf16),
            pltpu.VMEM((rows, width), bf16),
            pltpu.VMEM((rows, xs * width), bf16),
            pltpu.VMEM((rows, xs * width), bf16),
            pltpu.VMEM((8, tokens), f32),
            pltpu.VMEM((xs, 8, tokens), f32),
            [pltpu.VMEM((rows, size), bf16) for _, _, size in chunks],
            [pltpu.VMEM((rows, size), bf16) for _, _, size in chunks],
            [pltpu.VMEM((tokens, size), bf16) for _, _, size in chunks[:-1]]
            + [pltpu.VMEM((8, tokens), f32)],
            [pltpu.VMEM((tokens, size), bf16) for _, _, size in chunks[:-1]]
            + [pltpu.VMEM((SIDE, 8, tokens), f32)],
            dma((5,)),
            dma((2, 2)),
            dma,
            dma,
            dma((2,)),
            dma((2,)),
            dma,
            dma((SIDE,)),
        ]
        + [dma] * 4
        + [dma((count,))] * 4,
        compiler_params=pltpu.CompilerParams(
            collective_id=0, has_side_effects=True, vmem_limit_bytes=24 * 1024 * 1024
        ),
    )(
        *[
            pltpu.with_memory_space_constraint(operand, pltpu.HBM)
            for operand in (
                ids.T,
                gates.T,
                hidden.reshape(routes, width),
                jnp.transpose(scale8, (2, 0, 1)),
                scale4,
                code8,
                code4,
            )
        ]
    )
    return mixed, token.reshape(tok), ratio.reshape(1)


def solution(mesh):
    experts, xs = mesh.shape["expert"], mesh.shape["tensor"]
    assert experts == SIDE * SIDE * CORES

    def run(hidden, *rest):
        tok, top = hidden.shape[0] // experts, hidden.shape[1]
        mapped = jax.shard_map(
            functools.partial(per_device, (xs, tok, top)),
            mesh=mesh,
            in_specs=(
                P("expert", None, "tensor"),
                P("expert", None),
                P("expert", None),
                P("expert", None, "tensor"),
                P("expert", None, "tensor"),
                P("expert", None, "tensor"),
                P("expert", None, "tensor"),
            ),
            out_specs=(P("expert", "tensor"), P("expert"), P("expert")),
            check_vma=False,
        )
        return mapped(hidden, *rest)

    return run
```

```python
import functools

import jax
import jax.numpy as jnp
from jax import lax
from jax.experimental import pallas as pl
from jax.experimental.pallas import tpu as pltpu
from jax.sharding import PartitionSpec as P

BLOCK = 128
SLOTS = 2
SIDE = 8
CORES = 2
EARLY = 2
MESH = pl.DeviceIdType.MESH
f32, bf16 = jnp.float32, jnp.bfloat16


def iota(shape, dim):
    return lax.broadcasted_iota(jnp.int32, shape, dim)


def dot(a, b):
    return jnp.dot(a, b, preferred_element_type=f32)


def split3(value):
    high = value.astype(bf16).astype(f32)
    rest = value - high
    middle = rest.astype(bf16).astype(f32)
    return high, middle, rest - middle


def chunks_of(width):
    full = 2 * BLOCK
    starts = [0] + list(range(width % full or full, width, full))
    ends = starts[1:] + [width]
    chunks = [(1 - n % 2, a, b - a) for n, (a, b) in enumerate(zip(starts, ends))]
    return chunks + [(1, width, BLOCK)]


class Path:
    def __init__(self, number, me):
        rest = lax.rem(me, SIDE * CORES)
        z, y, core = me // (SIDE * CORES), rest // CORES, lax.rem(rest, CORES)
        self.number, self.core = number, core
        self.place, self.other = (z, y) if number == 0 else (y, z)
        self.spot = self.other * CORES + core

    def column(self, there):
        if self.number == 0:
            return there * (SIDE * CORES) + self.spot
        return self.other * (SIDE * CORES) + there * CORES + self.core

    def row(self, there):
        if self.number == 0:
            return self.place * (SIDE * CORES) + there
        return there // CORES * (SIDE * CORES) + self.place * CORES + lax.rem(there, CORES)


def far_first(d, count):
    step = d // 2
    return count // 2 + jnp.where(d % 2 == 1, -step, step)


def kernel(
    sizes,
    ids_hbm, gate_hbm, hidden_hbm, scale8_hbm, scale4_hbm, code8_hbm, code4_hbm,
    mixed_ref, token_ref, ratio_ref,
    ids_ref, gate_ref, hidden_ref, scale8_ref, scale4_ref, w8, w4, send1, gates1, recv1, grecv,
    send2, x_all, x_turned, sums, sums_all, outs, backs, parts, ends,
    small_sem, code_sem, s1, r1, sg, rg, s2, r2, sx, rx, se, re, sb, rb, sc, rc,
):
    xs, tok, top = sizes
    routes = tok * top
    spots = SIDE * CORES
    rows = SIDE * spots * SLOTS
    c_rows, r_rows = spots * SLOTS, SIDE * SLOTS
    tokens = SIDE * tok
    width = hidden_ref.shape[1]
    inner, feats = w8.shape
    chunks = chunks_of(feats)
    last = len(chunks) - 1

    me, tn = lax.axis_index("expert"), lax.axis_index("tensor")
    paths = Path(0, me), Path(1, me)
    first = paths[0]

    def in_column(path, d):
        return lax.rem(path.place + far_first(d, SIDE), SIDE)

    def in_row(path, d):
        return lax.rem(path.spot + far_first(d, spots), spots)

    def in_gather(d):
        return lax.rem(tn + d, xs)

    barrier = pltpu.get_barrier_semaphore()

    def signal(device):
        pl.semaphore_signal(barrier, inc=1, device_id=device, device_id_type=MESH)

    @pl.loop(1, SIDE)
    def _(d):
        for path in paths:
            step = in_column(path, d) * CORES
            for core in range(CORES):
                signal({"expert": paths[1 - path.number].row(step + core)})

    signal({"expert": first.row(first.other * CORES + 1 - first.core)})

    @pl.loop(1, xs)
    def _(d):
        signal({"tensor": in_gather(d)})

    small = (
        (ids_hbm, ids_ref),
        (gate_hbm, gate_ref),
        (hidden_hbm, hidden_ref),
        (scale8_hbm, scale8_ref),
        (scale4_hbm, scale4_ref),
    )
    small_copies = []
    for n, (src, dst) in enumerate(small):
        copy = pltpu.make_async_copy(src, dst, small_sem.at[n])
        copy.start()
        small_copies.append(copy)
    part_rows = inner // 2
    code_copies = []
    for n, (src, dst) in enumerate(((code8_hbm, w8), (code4_hbm, w4))):
        for h in range(2):
            piece = pl.ds(h * part_rows, part_rows)
            copy = pltpu.make_async_copy(src.at[0, piece, :], dst.at[piece, :], code_sem.at[n, h])
            copy.start()
            code_copies.append(copy)

    for copy in small_copies[:3]:
        copy.wait()
    gate = gate_ref[...]
    high = gate.astype(bf16).astype(f32)
    table = jnp.concatenate([ids_ref[...].astype(f32), high, gate - high], axis=0).astype(bf16)
    repeat = (iota((tok, routes), 0) == iota((tok, routes), 1) // top).astype(f32).astype(bf16)
    table = dot(table, repeat)
    own_choice = iota((top, routes), 0) == iota((top, routes), 1) % top

    def flat(n):
        rows_of = table[n * top : (n + 1) * top]
        return jnp.sum(jnp.where(own_choice, rows_of, 0.0), axis=0, keepdims=True)

    flat_ids, gate_high, gate_low = flat(0), flat(1), flat(2)
    ids = jnp.broadcast_to(flat_ids, (routes, routes))
    earlier = (ids == ids.T) & (iota((routes, routes), 0) < iota((routes, routes), 1))
    position = jnp.sum(jnp.where(earlier, 1.0, 0.0), axis=0, keepdims=True).astype(jnp.int32)
    expert = flat_ids.astype(jnp.int32)
    target = expert % spots * r_rows + expert // spots * SLOTS + position
    chosen = iota((rows, routes), 0) == target
    send1[...] = dot(chosen.astype(f32).astype(bf16), hidden_ref[...]).astype(bf16)

    pl.semaphore_wait(barrier, 2 * (SIDE - 1) + spots - 1 + xs - 1)

    def copy_to(device, src, dst, send, recv):
        return pltpu.make_async_remote_copy(
            src_ref=src,
            dst_ref=dst,
            send_sem=send,
            recv_sem=recv,
            device_id=device,
            device_id_type=MESH,
        )

    here = {"expert": me}

    def c_block(n):
        return pl.ds(pl.multiple_of(n * c_rows, c_rows), c_rows)

    def r_block(n):
        return pl.ds(pl.multiple_of(n * r_rows, r_rows), r_rows)

    def t_block(n):
        return pl.ds(pl.multiple_of(n * tok, tok), tok)

    def row_exchange(path, src, dst, send, recv):
        @pl.loop(1, spots)
        def _(d):
            there = in_row(path, d)
            copy_to(
                {"expert": path.row(there)},
                src.at[r_block(there)],
                dst.at[r_block(path.spot)],
                send,
                recv,
            ).start()

    def column_exchange(path, src, dst, send, recv):
        @pl.loop(1, SIDE)
        def _(d):
            there = in_column(path, d)
            copy_to(
                {"expert": path.column(there)},
                src.at[c_block(there)],
                dst.at[c_block(path.place)],
                send,
                recv,
            ).start()

    row_exchange(first, send1, recv1, s1, r1)
    recv1[r_block(first.spot), :] = send1[r_block(first.spot), :]

    lanes = gates1.shape[2]
    token_of = iota((routes, lanes), 0) // top
    lane = iota((routes, lanes), 1)
    spread_high = (lane == token_of).astype(f32).astype(bf16)
    spread_low = (lane == token_of + tok).astype(f32).astype(bf16)
    turned = expert // CORES % SIDE * c_rows + expert // spots * CORES * SLOTS
    turned = turned + expert % CORES * SLOTS + position
    for path, target in zip(paths, (expert * SLOTS + position, turned)):
        chosen = iota((rows, routes), 0) == target
        gates = dot(jnp.where(chosen, gate_high, 0.0).astype(bf16), spread_high)
        gates = gates + dot(jnp.where(chosen, gate_low, 0.0).astype(bf16), spread_low)
        gates1[path.number] = gates.astype(bf16)

    def scale_weights(begin, end):
        @pl.loop(begin, end)
        def _(g):
            group = pl.ds(pl.multiple_of(g * BLOCK, BLOCK), BLOCK)
            for b in range(feats // BLOCK):
                cols = pl.ds(b * BLOCK, BLOCK)
                w8[group, cols] = (w8[group, cols].astype(f32) * scale8_ref[b, 0, g]).astype(bf16)
            w4[group, :] = (w4[group, :].astype(f32) * scale4_ref[0, pl.ds(g, 1), :]).astype(bf16)

    groups = inner // BLOCK
    for copy in small_copies[3:] + code_copies:
        copy.wait()
    scale_weights(0, groups)

    at, of = iota((rows, rows), 0), iota((rows, rows), 1)
    low_place, slot = at % r_rows // SLOTS, at % SLOTS
    reorder = of == low_place * c_rows + at // r_rows * SLOTS + slot
    reorder = reorder.astype(f32).astype(bf16)
    turn = of == low_place * c_rows + at % c_rows // r_rows * r_rows + at // c_rows * SLOTS + slot
    turn = turn.astype(f32).astype(bf16)

    but_c, but_r = pl.ds(0, rows - c_rows), pl.ds(0, rows - r_rows)
    wait_1 = copy_to(here, send1.at[but_r], recv1.at[but_r], s1, r1)
    wait_1.wait_recv()
    send2[...] = dot(turn, recv1[...]).astype(bf16)

    mine = pl.ds(pl.multiple_of(tn * width, width), width)
    arrived = x_all.at[:, mine]
    column_exchange(first, send2, arrived, s2, r2.at[first.place])
    x_all[c_block(first.place), mine] = send2[c_block(first.place), :]
    for path in paths:
        n = path.number
        column_exchange(path, gates1.at[n], grecv.at[n], sg.at[n], rg.at[n])
        grecv[n, c_block(path.place), :] = gates1[n, c_block(path.place), :]

    for n in range(SIDE):
        step = n // 2 if n % 2 == 0 else -(n // 2 + 1)
        source = lax.rem(first.place + SIDE + step, SIDE)
        block = c_block(source)
        if n > 0:
            copy_to(here, send2.at[block], arrived.at[block], s2, r2.at[source]).wait_recv()

        @pl.loop(1, xs)
        def _(d):
            copy_to(
                {"tensor": in_gather(d)}, arrived.at[block], arrived.at[block], sx, rx
            ).start()

    wait_2 = copy_to(here, send2.at[but_c], arrived.at[but_c], s2, r2.at[0])

    place, wide = iota((lanes, 2 * tokens), 0), iota((lanes, 2 * tokens), 1)
    widen = (place == wide % tok + jnp.where(wide < tokens, 0, tok)).astype(f32).astype(bf16)
    row_place = iota((rows, 2 * tokens), 0) % r_rows // SLOTS
    own_place = row_place == iota((rows, 2 * tokens), 1) % tokens // tok
    combine, waits_g = [], []
    for path in paths:
        n = path.number
        wait_g = copy_to(here, gates1.at[n, but_c], grecv.at[n, but_c], sg.at[n], rg.at[n])
        wait_g.wait_recv()
        waits_g.append(wait_g)
        gates = dot(dot(reorder, grecv[n]).astype(bf16), widen)
        combine.append(jnp.where(own_place, gates, 0.0).T.astype(bf16))

    others = pl.ds(0, (xs - 1) * width)
    wait_x = copy_to(here, x_all.at[:, others], x_all.at[:, others], sx, rx)
    wait_x.wait_recv()

    def send_back(c):
        path = paths[chunks[c][0]]

        @pl.loop(1, spots)
        def _(d):
            there = in_row(path, d)
            copy_to(
                {"expert": path.row(there)},
                outs[c].at[r_block(there)],
                backs[c].at[r_block(path.spot)],
                sb.at[c],
                rb.at[c],
            ).start()

        backs[c][r_block(path.spot), :] = outs[c][r_block(path.spot), :]

    early = min(EARLY, last)
    for c, (number, start, size) in enumerate(chunks[:last]):
        if c == 1:
            x_turned[...] = dot(turn, x_all[...]).astype(bf16)
        activation = x_all if number else x_turned
        outs[c][...] = dot(activation[...], w8[:, start : start + size]).astype(bf16)
        if c < early:
            send_back(c)
    gap_sums = [jnp.zeros((rows, BLOCK), f32), jnp.zeros((rows, BLOCK), f32)]
    ref_sum = jnp.zeros((rows, BLOCK), f32)
    for c, (number, start, size) in enumerate(chunks[:last]):
        activation = x_all if number else x_turned
        result4 = dot(activation[...], w4[:, start : start + size]).astype(bf16).astype(f32)
        result8 = outs[c][...].astype(f32)
        gap = result4 - result8
        for b in range(size // BLOCK):
            cols = slice(b * BLOCK, (b + 1) * BLOCK)
            gap_sums[number] += gap[:, cols] * gap[:, cols]
            ref_sum += result8[:, cols] * result8[:, cols]

    def stack3(value, count):
        high, middle, low = split3(value)
        which = iota((count, rows), 0)
        low = jnp.where(which == 2, low, 0.0)
        return jnp.where(which == 0, high, jnp.where(which == 1, middle, low)).astype(bf16)

    gap_rows = [jnp.sum(gap_sum.T, axis=0, keepdims=True) for gap_sum in gap_sums]
    last_path = chunks[last][0]
    moved = jnp.sum(dot(stack3(gap_rows[1 - last_path], 8), turn), axis=0, keepdims=True)
    gap_row = gap_rows[last_path] + moved
    outs[last][...] = stack3(gap_row, BLOCK).astype(f32).T.astype(bf16)
    for c in [last] + list(range(early, last)):
        send_back(c)
    gap_part = jnp.sum(gap_row, axis=1, keepdims=True)
    ref_part = jnp.sum(jnp.sum(ref_sum, axis=0, keepdims=True), axis=1, keepdims=True)

    def wait_back(c):
        return copy_to(here, outs[c].at[but_r], backs[c].at[but_r], sb.at[c], rb.at[c])

    def wait_end(c):
        some = pl.ds(0, SIDE - 1) if c == last else pl.ds(0, tokens - tok)
        return copy_to(here, ends[c].at[some], ends[c].at[some], sc.at[c], rc.at[c])

    def combine_and_send(c):
        path = paths[chunks[c][0]]
        wait_back(c).wait_recv()
        both = dot(combine[path.number], backs[c][...])
        total = both[:tokens] + both[tokens:]
        if c == last:
            error = jnp.sum(total, axis=1, keepdims=True)
            parts[c][...] = jnp.broadcast_to(error, (tokens, BLOCK)).T[:8]
        else:
            parts[c][...] = total.astype(bf16)

        @pl.loop(1, SIDE)
        def _(d):
            there = in_column(path, d)
            copy_to(
                {"expert": path.column(there)},
                parts[c] if c == last else parts[c].at[t_block(there)],
                ends[c].at[path.place] if c == last else ends[c].at[t_block(path.place)],
                sc.at[c],
                rc.at[c],
            ).start()

        if c == last:
            ends[c][path.place] = parts[c][...]
        else:
            ends[c][t_block(path.place), :] = parts[c][t_block(path.place), :]

    order = list(range(early)) + [last] + list(range(early, last))
    for c in order:
        combine_and_send(c)

    for c in order:
        wait_end(c).wait_recv()
        if c < last:
            _, start, size = chunks[c]
            total = ends[c][:tok].astype(f32)
            for n in range(1, SIDE):
                total = total + ends[c][n * tok : (n + 1) * tok].astype(f32)
            mixed_ref[:, start : start + size] = total.astype(bf16)
        else:
            total = ends[c][0]
            for n in range(1, SIDE):
                total = total + ends[c][n]
            which = iota((8, tokens), 0)
            sums[...] = jnp.where(which == 0, total, jnp.where(which == 1, gap_part, ref_part))
            sums_all[tn] = sums[...]

            @pl.loop(1, xs)
            def _(d):
                copy_to({"tensor": in_gather(d)}, sums, sums_all.at[tn], se, re).start()

    sums_but = pl.ds(0, xs - 1)
    wait_e = copy_to(here, sums_all.at[sums_but], sums_all.at[sums_but], se, re)
    wait_e.wait_recv()
    total = sums_all[0]
    for n in range(1, xs):
        total = total + sums_all[n]
    ratio_ref[...] = total[1:2, :1] / (total[2:3, :1] + 1e-06)
    place = iota((tok, tokens), 1) - paths[chunks[last][0]].place * tok
    error = jnp.where(place == iota((tok, tokens), 0), total[0:1], 0.0)
    error = jnp.sum(error, axis=1, keepdims=True)
    diagonal = iota((tok, tok), 0) == iota((tok, tok), 1)
    token_ref[...] = jnp.sum(jnp.where(diagonal, error, 0.0), axis=0, keepdims=True)

    for wait in [wait_1, wait_2, wait_x, wait_e] + waits_g:
        wait.wait_send()
    for c in range(last + 1):
        wait_back(c).wait_send()
        wait_end(c).wait_send()


def per_device(sizes, hidden, ids, gates, code8, scale8, code4, scale4):
    xs, tok, top = sizes
    routes, width = tok * top, hidden.shape[2]
    rows = SIDE * SIDE * CORES * SLOTS
    inner, feats = code8.shape[1:]
    chunks = chunks_of(feats)
    count, tokens = len(chunks), SIDE * tok
    vmem = pl.BlockSpec(memory_space=pltpu.VMEM)
    dma = pltpu.SemaphoreType.DMA
    mixed, token, ratio = pl.pallas_call(
        functools.partial(kernel, sizes),
        out_shape=(
            jax.ShapeDtypeStruct((tok, feats), bf16),
            jax.ShapeDtypeStruct((1, tok), f32),
            jax.ShapeDtypeStruct((1, 1), f32),
        ),
        in_specs=[pl.BlockSpec(memory_space=pltpu.HBM)] * 7,
        out_specs=(vmem, vmem, vmem),
        scratch_shapes=[
            pltpu.VMEM((top, tok), jnp.int32),
            pltpu.VMEM((top, tok), f32),
            pltpu.VMEM((routes, width), bf16),
            pltpu.SMEM((feats // BLOCK, 1, inner // BLOCK), f32),
            pltpu.VMEM((1, inner // BLOCK, feats), f32),
            pltpu.VMEM((inner, feats), bf16),
            pltpu.VMEM((inner, feats), bf16),
            pltpu.VMEM((rows, width), bf16),
            pltpu.VMEM((2, rows, BLOCK), bf16),
            pltpu.VMEM((rows, width), bf16),
            pltpu.VMEM((2, rows, BLOCK), bf16),
            pltpu.VMEM((rows, width), bf16),
            pltpu.VMEM((rows, xs * width), bf16),
            pltpu.VMEM((rows, xs * width), bf16),
            pltpu.VMEM((8, tokens), f32),
            pltpu.VMEM((xs, 8, tokens), f32),
            [pltpu.VMEM((rows, size), bf16) for _, _, size in chunks],
            [pltpu.VMEM((rows, size), bf16) for _, _, size in chunks],
            [pltpu.VMEM((tokens, size), bf16) for _, _, size in chunks[:-1]]
            + [pltpu.VMEM((8, tokens), f32)],
            [pltpu.VMEM((tokens, size), bf16) for _, _, size in chunks[:-1]]
            + [pltpu.VMEM((SIDE, 8, tokens), f32)],
            dma((5,)),
            dma((2, 2)),
            dma,
            dma,
            dma((2,)),
            dma((2,)),
            dma,
            dma((SIDE,)),
        ]
        + [dma] * 4
        + [dma((count,))] * 4,
        compiler_params=pltpu.CompilerParams(
            collective_id=0, has_side_effects=True, vmem_limit_bytes=24 * 1024 * 1024
        ),
    )(
        *[
            pltpu.with_memory_space_constraint(operand, pltpu.HBM)
            for operand in (
                ids.T,
                gates.T,
                hidden.reshape(routes, width),
                jnp.transpose(scale8, (2, 0, 1)),
                scale4,
                code8,
                code4,
            )
        ]
    )
    return mixed, token.reshape(tok), ratio.reshape(1)


def solution(mesh):
    experts, xs = mesh.shape["expert"], mesh.shape["tensor"]
    assert experts == SIDE * SIDE * CORES

    def run(hidden, *rest):
        tok, top = hidden.shape[0] // experts, hidden.shape[1]
        mapped = jax.shard_map(
            functools.partial(per_device, (xs, tok, top)),
            mesh=mesh,
            in_specs=(
                P("expert", None, "tensor"),
                P("expert", None),
                P("expert", None),
                P("expert", None, "tensor"),
                P("expert", None, "tensor"),
                P("expert", None, "tensor"),
                P("expert", None, "tensor"),
            ),
            out_specs=(P("expert", "tensor"), P("expert"), P("expert")),
            check_vma=False,
        )
        return mapped(hidden, *rest)

    return run
```
